512 devices in a mesh: rep: 16 (over x_hi, y, core), tp: 32 (over x_lo, z).
Axes of the slice: x: 4 (x_hi: 2, x_lo: 2; x = x_hi * 2 + x_lo), y: 4, z: 16, core: 2. Of those that a mesh axis runs over, the one named last changes fastest.
Arguments:
- hidden_old: bfloat16 [2, 1024, 8192], P(None, 'rep', 'tp'), parts along dimension 1, may hold values from -6 to 6
- queries_old: bfloat16 [16384, 8, 128], P(('rep', 'tp')), parts along dimension 0, may hold values from -25 to 25
- kv_weight: bfloat16 [8192, 4096], P(None, 'tp'), may hold values from -0.0625 to 0.0625
- cache: bfloat16 [16384, 64, 256], P(('rep', 'tp')), parts along dimension 0, may hold values from -6 to 6
- lengths: int32 [1024], P('rep'), parts along dimension 0, may hold values from 2 to 63, as said below
- slot: int32 [1024], P('rep'), parts along dimension 0, may hold values from 0 to 63, as said below
- hidden_new: bfloat16 [2, 1024, 8192], P(None, 'rep', 'tp'), parts along dimension 1, may hold values from -6 to 6
- queries_new: bfloat16 [1024, 128, 128], P(('rep', 'tp')), parts along dimension 0, may hold values from -25 to 25
Outputs:
- attended_old: bfloat16 [16384, 8, 128], P(('rep', 'tp')), parts along dimension 0
- attended_new: bfloat16 [1024, 128, 128], P(('rep', 'tp')), parts along dimension 0
- served: bfloat16 [1024, 1024, 256], P(('rep', 'tp')), parts along dimension 0
The draws below stay inside these ranges and needn't reach their ends.
There are 16 independent parts, one for each index of `rep`. The reference program is written for one: setup_inputs(seed, part) draws one part's arguments, and reference() takes and returns one part's arrays. A program takes and returns all parts, laid end to end along the dimension named above; an argument that names none is the same for every part. Nothing has to cross between parts.
Inputs may be any that keep to these rules, and one draw needn't show every extreme that they name: `lengths`: in every draw one sequence has 63 filled positions and another has 2. `slot`: a permutation in which sequences r < 32 take even positions and the others odd positions.
All inputs are finite; a program needn't handle non-finite values.
Results may differ from the reference program's by a relative error of at most 0.0065.
Values may be sent and summed in bfloat16 or wider, within the bound.
A program may use at most 64 MiB of HBM per device.

```python
import jax
import jax.numpy as jnp
from jax import lax

D = 8192
KVH = 8
HD = 128
GROUP = 8
ROWS = 64
CTX = 64


def draw_queries_old(key, part):
    key = jax.random.fold_in(key, 1)
    split_one = jax.random.fold_in(key, 0)
    values = jnp.clip(jax.random.normal(split_one, (2 * KVH, ROWS, GROUP, HD), jnp.float32), -6.0, 6.0)
    return values.reshape(2 * KVH * ROWS, GROUP, HD).astype(jnp.bfloat16)


def draw_queries_new(key, part):
    key = jax.random.fold_in(key, 2)
    split_one = jax.random.fold_in(key, 0)
    values = jnp.clip(jax.random.normal(split_one, (ROWS, 2 * KVH, GROUP, HD), jnp.float32), -6.0, 6.0)
    return values.reshape(ROWS, 2 * KVH * GROUP, HD).astype(jnp.bfloat16)


def draw_cache(key, part):
    key = jax.random.fold_in(key, 3)
    values = jnp.clip(jax.random.normal(key, (2 * KVH, ROWS, CTX, 2 * HD), jnp.float32), -6.0, 6.0)
    return values.reshape(2 * KVH * ROWS, CTX, 2 * HD).astype(jnp.bfloat16)


def draw_lengths(key, part):
    key = jax.random.fold_in(key, 5)
    split_one, split_two, split_three = jax.random.split(key, 3)
    drawn_len = jax.random.randint(split_one, (ROWS,), 2, CTX)
    longest = jax.random.randint(split_two, (), 0, ROWS)
    shortest = (longest + 1 + jax.random.randint(split_three, (), 0, ROWS - 1)) % ROWS
    row_ids = jnp.arange(ROWS)
    drawn_len = jnp.where(row_ids == longest, CTX - 1, drawn_len)
    drawn_len = jnp.where(row_ids == shortest, 2, drawn_len)
    return drawn_len.astype(jnp.int32)


def draw_slot(key, part):
    key = jax.random.fold_in(key, 6)
    split_one, split_two = jax.random.split(key)
    even_slots = 2 * jax.random.permutation(split_one, ROWS // 2)
    odd_slots = 2 * jax.random.permutation(split_two, ROWS // 2) + 1
    return jnp.concatenate([even_slots, odd_slots]).astype(jnp.int32)


def level_of(key, dims, shards, smallest, high):
    gain = 1.0
    for dim, parts in shards:
        steps = jax.random.uniform(jax.random.fold_in(jax.random.fold_in(key, 6), dim), (parts,), jnp.float32, smallest / len(shards), high / len(shards))
        gain = gain * jnp.repeat(jnp.exp(steps), dims[dim] // parts).reshape((-1,) + (1,) * (len(dims) - 1 - dim))
    return gain


def noise(own_key, dims, spread, most, cuts=(), kind=jnp.bfloat16):
    result = spread * jax.random.normal(own_key, dims, jnp.float32)
    if cuts:
        result = result * level_of(own_key, dims, cuts, -0.22, 0.18)
    return jnp.clip(result, -most, most).astype(kind)


def setup_inputs(seed: int = 0, part: int = 0) -> dict:
    key_of = jax.random.split(jax.random.key(seed), 9)
    part_keys = jax.random.split(jax.random.fold_in(key_of[8], part), 9)
    hidden_old = noise(part_keys[0], (2, ROWS, D), 1.0, 6.0, ((2, 32),))
    queries_old = draw_queries_old(jax.random.fold_in(jax.random.fold_in(key_of[8], part), 71), part)
    kv_weight = noise(key_of[2], (D, 4 * KVH * HD), D ** -0.5, 0.0625, ((1, 32),))
    cache = draw_cache(jax.random.fold_in(jax.random.fold_in(key_of[8], part), 71), part)
    lengths = draw_lengths(jax.random.fold_in(jax.random.fold_in(key_of[8], part), 71), part)
    slot = draw_slot(jax.random.fold_in(jax.random.fold_in(key_of[8], part), 71), part)
    hidden_new = noise(part_keys[6], (2, ROWS, D), 1.0, 6.0, ((2, 32),))
    queries_new = draw_queries_new(jax.random.fold_in(jax.random.fold_in(key_of[8], part), 71), part)
    return {"hidden_old": hidden_old, "queries_old": queries_old, "kv_weight": kv_weight, "cache": cache, "lengths": lengths, "slot": slot, "hidden_new": hidden_new, "queries_new": queries_new}


def attend(queries, key_rows, value_rows, own_keys, own_values, valid_mask):
    score_scale = 1.0 / (HD ** 0.5)
    query_f = queries.astype(jnp.float32)
    scores = jnp.einsum("abge,able->abgl", query_f, key_rows.astype(jnp.float32)) * score_scale
    own_score = jnp.einsum("abge,abe->abg", query_f, own_keys.astype(jnp.float32)) * score_scale
    scores = jnp.where(valid_mask[:, :, None, :], scores, -jnp.inf)
    row_max = jnp.maximum(jnp.max(scores, axis=-1), own_score)
    weights = jnp.exp(scores - row_max[..., None])
    own_weight = jnp.exp(own_score - row_max)
    row_total = jnp.sum(weights, axis=-1) + own_weight
    weights = (weights / row_total[..., None]).astype(jnp.bfloat16)
    own_weight = (own_weight / row_total).astype(jnp.bfloat16)
    attended = jnp.einsum("abgl,able->abge", weights.astype(jnp.float32), value_rows.astype(jnp.float32))
    attended = attended + own_weight.astype(jnp.float32)[..., None] * own_values.astype(jnp.float32)[:, :, None, :]
    return attended.astype(jnp.bfloat16)


def project(hidden, kv_weight):
    layer_cols = 2 * KVH * HD
    pieces = []
    for layer_no in range(2):
        pieces.append(jnp.dot(hidden[layer_no], kv_weight[:, layer_no * layer_cols:(layer_no + 1) * layer_cols],
                              preferred_element_type=jnp.float32).astype(jnp.bfloat16))
    return jnp.concatenate(pieces, axis=1)


def reference(hidden_old, queries_old, kv_weight, cache, lengths, slot, hidden_new, queries_new):
    heads_all = 2 * KVH
    fresh_old = jnp.transpose(project(hidden_old, kv_weight).reshape(ROWS, heads_all, 2 * HD), (1, 0, 2))
    stored = cache.reshape(heads_all, ROWS, CTX, 2 * HD)
    position = lax.broadcasted_iota(jnp.int32, (ROWS, CTX), 1)
    valid_old = (position < lengths[:, None])[None]
    attended_old = attend(queries_old.reshape(heads_all, ROWS, GROUP, HD), stored[..., :HD], stored[..., HD:],
                          fresh_old[..., :HD], fresh_old[..., HD:], valid_old)
    attended_old = attended_old.reshape(heads_all * ROWS, GROUP, HD)
    landing = (position == lengths[:, None])[None, :, :, None]
    appended = jnp.where(landing, fresh_old[:, :, None, :], stored)
    order_rows = jnp.zeros((ROWS,), jnp.int32).at[slot].set(jnp.arange(ROWS, dtype=jnp.int32))
    served = jnp.transpose(jnp.take(appended, order_rows, axis=1), (1, 0, 2, 3))
    served_len = jnp.take(lengths, order_rows) + 1
    fresh_new = project(hidden_new, kv_weight).reshape(ROWS, heads_all, 2 * HD)
    valid_new = (position < served_len[:, None])[:, None, :]
    attended_new = attend(queries_new.reshape(ROWS, heads_all, GROUP, HD), served[..., :HD], served[..., HD:],
                          fresh_new[..., :HD], fresh_new[..., HD:], valid_new)
    attended_new = attended_new.reshape(ROWS, heads_all * GROUP, HD)
    return (attended_old, attended_new, served.reshape(ROWS, heads_all * CTX, 2 * HD))
```

```python
import jax
import jax.numpy as jnp
from jax import lax
from jax.experimental import pallas as pl
from jax.experimental.pallas import tpu as pltpu
from jax.sharding import PartitionSpec as P

MESH = pl.DeviceIdType.MESH
TP = 32
NZ = 16


def remote(src, dst, send_sem, recv_sem, target):
    return pltpu.make_async_remote_copy(
        src_ref=src,
        dst_ref=dst,
        send_sem=send_sem,
        recv_sem=recv_sem,
        device_id={"tp": target},
        device_id_type=MESH,
    )


def exchange_kernel(
    order_ref,
    key_ref,
    hold_ref,
    hnew_ref,
    w_hbm,
    cache_hbm,
    raw_ref,
    fresh_ref,
    pair_ref,
    hbuf,
    wbuf,
    cbuf,
    sbuf,
    mbuf,
    obuf,
    acc,
    local_sem,
    xs_sem,
    xr_sem,
    gs_sem,
    gr_sem,
    cs_sem,
    cr_sem,
    ms_sem,
    mr_sem,
    ps_sem,
    pr_sem,
):
    me = lax.axis_index("tp")
    x = me // NZ
    z = me % NZ
    other = 1 - x
    half = z % 2
    head = me // 2

    load_own = [
        pltpu.make_async_copy(hold_ref.at[x], hbuf.at[z, x, pl.ds(0, 64)], local_sem.at[0]),
        pltpu.make_async_copy(hnew_ref.at[x], hbuf.at[z, x, pl.ds(64, 64)], local_sem.at[1]),
    ]
    load_w = pltpu.make_async_copy(w_hbm, wbuf, local_sem.at[2])
    load_c = pltpu.make_async_copy(cache_hbm, cbuf, local_sem.at[3])
    for c in load_own:
        c.start()
    load_c.start()
    load_w.start()

    barrier = pltpu.get_barrier_semaphore()
    for d in range(1, TP):
        pl.semaphore_signal(barrier, inc=1, device_id={"tp": (me + d) % TP}, device_id_type=MESH)
    pl.semaphore_wait(barrier, TP - 1)

    twin = other * NZ + z
    xcopies = [
        remote(hold_ref.at[other], hbuf.at[z, x, pl.ds(0, 64)], xs_sem.at[0], xr_sem.at[0], twin),
        remote(hnew_ref.at[other], hbuf.at[z, x, pl.ds(64, 64)], xs_sem.at[1], xr_sem.at[1], twin),
    ]
    for c in xcopies:
        c.start()

    right = x * NZ + (z + 1) % NZ
    left = x * NZ + (z + NZ - 1) % NZ
    steps = ((8, 7), (7, 8))
    planes = (x, other)
    sent = []

    def ring(stream, way, k):
        slot = (z + (NZ - k if way == 0 else k)) % NZ
        block = hbuf.at[slot, planes[stream]]
        where = (stream * 2 + way) * 8 + k
        return remote(block, block, gs_sem.at[where], gr_sem.at[where], right if way == 0 else left)

    def multiply(stream, slot):
        plane = planes[stream]
        rows = pl.ds(pl.multiple_of((plane * NZ + slot) * 256, 256), 256)
        acc[...] += jnp.dot(
            hbuf[slot, plane], wbuf[rows, :], preferred_element_type=jnp.float32
        )

    offsets = []
    for dz in (8, 7, 9, 6, 10, 5, 11, 4, 12, 3, 13, 2, 14, 1, 15, 0):
        for dx in (0, 1):
            if dz or dx:
                offsets.append((dx, dz))
    cache_copies = []

    def send_block(j):
        dx, dz = offsets[j]
        target = (x + dx) % 2 * NZ + (z + dz) % NZ
        sbuf[j] = cbuf[order_ref[target]]
        c = remote(sbuf.at[j], raw_ref.at[half, head], cs_sem.at[j], cr_sem.at[j], target)
        c.start()
        cache_copies.append(c)

    acc[...] = jnp.zeros_like(acc)
    for c in load_own:
        c.wait()
    for way in range(2):
        c = ring(0, way, 0)
        c.start()
        sent.append(c)
    for c in xcopies:
        c.wait_recv()
    for way in range(2):
        c = ring(1, way, 0)
        c.start()
        sent.append(c)
    load_c.wait()
    for j in range(4):
        send_block(j)
    load_w.wait()
    multiply(0, z)
    multiply(1, z)
    done = 4
    for k in range(8):
        for stream in range(2):
            for way in range(2):
                if k >= steps[stream][way]:
                    continue
                ring(stream, way, k).wait_recv()
                if k + 1 < steps[stream][way]:
                    c = ring(stream, way, k + 1)
                    c.start()
                    sent.append(c)
                multiply(stream, (z + (NZ - k - 1 if way == 0 else k + 1)) % NZ)
        for j in range(done, min(done + 4, len(offsets))):
            send_block(j)
        done = min(done + 4, len(offsets))

    fresh = acc[...].astype(jnp.bfloat16)
    rid = lax.broadcasted_iota(jnp.int32, (TP * 16, 128), 0)
    j = rid & 15
    d = rid >> 4
    wanted = jnp.where(j < 2, 2 * d + j, jnp.where(j < 4, 62 + 2 * d + j, -1))
    pick = (key_ref[...] == wanted).astype(jnp.bfloat16)
    messages = jnp.dot(pick, fresh, preferred_element_type=jnp.float32).astype(jnp.bfloat16)
    mbuf[...] = messages.reshape(TP, 16, 128)
    obuf[...] = fresh[:64].reshape(2, 32, 128)
    partner = x * NZ + z + 1 - 2 * half
    pcopy = remote(obuf.at[1 - half], pair_ref.at[half], ps_sem, pr_sem, partner)
    pcopy.start()
    message_copies = []
    for i in range(1, TP):
        target = (me + i) % TP
        c = remote(mbuf.at[target], fresh_ref.at[me], ms_sem.at[i], mr_sem.at[i], target)
        c.start()
        message_copies.append(c)
    pair_ref[half] = obuf[half]
    fresh_ref[me] = mbuf[me]
    sbuf[TP - 1] = cbuf[order_ref[me]]
    mine = pltpu.make_async_copy(sbuf.at[TP - 1], raw_ref.at[half, head], local_sem.at[4])
    mine.start()

    for c in sent:
        c.wait_send()
    for c in xcopies:
        c.wait_send()
    pcopy.wait()
    for c in message_copies:
        c.wait()
    for c in cache_copies:
        c.wait()
    mine.wait()


def exchange(order, key, hidden_old, hidden_new, kv_weight, cache):
    any_spec = pl.BlockSpec(memory_space=pl.ANY)
    vmem = pl.BlockSpec(memory_space=pltpu.VMEM)
    smem = pl.BlockSpec(memory_space=pltpu.SMEM)
    dma = pltpu.SemaphoreType.DMA
    bf = jnp.bfloat16
    return pl.pallas_call(
        exchange_kernel,
        out_shape=(
            jax.ShapeDtypeStruct((2, 16, 64, 256), bf),
            jax.ShapeDtypeStruct((TP, 16, 128), bf),
            jax.ShapeDtypeStruct((2, 32, 128), bf),
        ),
        in_specs=[smem, vmem, any_spec, any_spec, any_spec, any_spec],
        out_specs=(any_spec, vmem, vmem),
        scratch_shapes=[
            pltpu.VMEM((NZ, 2, 128, 256), bf),
            pltpu.VMEM((8192, 128), bf),
            pltpu.VMEM((32, 64, 256), bf),
            pltpu.VMEM((32, 64, 256), bf),
            pltpu.VMEM((TP, 16, 128), bf),
            pltpu.VMEM((2, 32, 128), bf),
            pltpu.VMEM((128, 128), jnp.float32),
            dma((5,)),
            dma((2,)),
            dma((2,)),
            dma((32,)),
            dma((32,)),
            dma((31,)),
            dma((31,)),
            dma((32,)),
            dma((32,)),
            dma,
            dma,
        ],
        compiler_params=pltpu.CompilerParams(
            collective_id=0, has_side_effects=True, vmem_limit_bytes=24 * 1024 * 1024
        ),
        cost_estimate=pl.CostEstimate(
            flops=2 * 128 * 8192 * 128, bytes_accessed=5 * 1024 * 1024, transcendentals=0
        ),
    )(order, key, hidden_old, hidden_new, kv_weight, cache)


def attend(queries, key_rows, value_rows, own_keys, own_values, valid_mask):
    score_scale = 1.0 / queries.shape[-1] ** 0.5
    scores = (
        jnp.einsum("abge,able->abgl", queries, key_rows, preferred_element_type=jnp.float32)
        * score_scale
    )
    own_score = (
        jnp.einsum("abge,abe->abg", queries, own_keys, preferred_element_type=jnp.float32)
        * score_scale
    )
    scores = jnp.where(valid_mask[:, :, None, :], scores, -jnp.inf)
    row_max = jnp.maximum(jnp.max(scores, axis=-1), own_score)
    weights = jnp.exp(scores - row_max[..., None])
    own_weight = jnp.exp(own_score - row_max)
    row_total = jnp.sum(weights, axis=-1) + own_weight
    weights = (weights / row_total[..., None]).astype(jnp.bfloat16)
    own_weight = (own_weight / row_total).astype(jnp.bfloat16)
    attended = jnp.einsum(
        "abgl,able->abge", weights, value_rows, preferred_element_type=jnp.float32
    )
    attended = (
        attended
        + own_weight.astype(jnp.float32)[..., None] * own_values.astype(jnp.float32)[:, :, None, :]
    )
    return attended.astype(jnp.bfloat16)


def shards(hidden_old, queries_old, kv_weight, cache, lengths, slot, hidden_new, queries_new):
    me = lax.axis_index("tp")
    half = me % 2
    first = half * 32
    my_slots = lax.dynamic_slice_in_dim(slot, first, 32)
    served_of = 2 * jnp.arange(TP, dtype=jnp.int32) + half
    hit = my_slots[None, :] == served_of[:, None]
    order = jnp.sum(jnp.where(hit, jnp.arange(32, dtype=jnp.int32)[None, :], 0), axis=1)
    key = jnp.concatenate([slot, jnp.arange(64, 128, dtype=jnp.int32)]).reshape(1, 128)
    raw, fresh, pair = exchange(order, key, hidden_old, hidden_new, kv_weight, cache)

    my_len = lax.dynamic_slice_in_dim(lengths, first, 32)
    position = lax.broadcasted_iota(jnp.int32, (32, 64), 1)
    valid_old = (position < my_len[:, None])[None]
    old_out = attend(
        queries_old[None],
        cache[None, ..., :128],
        cache[None, ..., 128:],
        pair[0][None],
        pair[1][None],
        valid_old,
    )
    attended_old = old_out.reshape(32, 8, 128)

    mine = 2 * me + jnp.arange(2, dtype=jnp.int32)
    new_len = jnp.sum(jnp.where(slot[None, :] == mine[:, None], lengths[None, :], 0), axis=1)
    landed = fresh[:, :4].reshape(16, 2, 2, 2, 128).transpose(2, 3, 0, 1, 4).reshape(2, 2, 16, 256)
    new_pos = lax.broadcasted_iota(jnp.int32, (2, 64), 1)
    landing = (new_pos == new_len[:, None])[:, None, :, None]
    served = jnp.where(landing, landed[0][:, :, None, :], raw)
    new_pairs = landed[1]
    valid_new = (new_pos < new_len[:, None] + 1)[:, None, :]
    new_out = attend(
        queries_new.reshape(2, 16, 8, 128),
        served[..., :128],
        served[..., 128:],
        new_pairs[..., :128],
        new_pairs[..., 128:],
        valid_new,
    )
    return (attended_old, new_out.reshape(2, 128, 128), served.reshape(2, 1024, 256))


def solution(mesh):
    placed = (
        P(None, "rep", "tp"),
        P(("rep", "tp"), None, None),
        P(None, "tp"),
        P(("rep", "tp"), None, None),
        P("rep"),
        P("rep"),
        P(None, "rep", "tp"),
        P(("rep", "tp"), None, None),
    )
    return jax.shard_map(
        shards,
        mesh=mesh,
        in_specs=placed,
        out_specs=(
            P(("rep", "tp"), None, None),
            P(("rep", "tp"), None, None),
            P(("rep", "tp"), None, None),
        ),
        check_vma=False,
    )
```

```python
import jax
import jax.numpy as jnp
from jax import lax
from jax.experimental import pallas as pl
from jax.experimental.pallas import tpu as pltpu
from jax.sharding import PartitionSpec as P

MESH = pl.DeviceIdType.MESH
TP = 32
NZ = 16
SCALE = 1.0 / 128.0**0.5


def remote(src, dst, send_sem, recv_sem, target):
    return pltpu.make_async_remote_copy(
        src_ref=src,
        dst_ref=dst,
        send_sem=send_sem,
        recv_sem=recv_sem,
        device_id={"tp": target},
        device_id_type=MESH,
    )


def stored_part(queries, block, limit):
    keys = block[:, :, :128]
    values = block[:, :, 128:]
    scores = (
        jnp.einsum("egd,eld->egl", queries, keys, preferred_element_type=jnp.float32) * SCALE
    )
    position = lax.broadcasted_iota(jnp.int32, scores.shape, 2).astype(jnp.float32)
    scores = jnp.where(position < limit, scores, -jnp.inf)
    top = jnp.max(scores, axis=-1, keepdims=True)
    weights = jnp.exp(scores - top)
    total = jnp.sum(weights, axis=-1, keepdims=True)
    mixed = jnp.einsum(
        "egl,eld->egd", weights.astype(jnp.bfloat16), values, preferred_element_type=jnp.float32
    )
    return mixed, top, total


def with_tokens(queries, stored, tokens):
    mixed, top, total = stored
    query_f = queries.astype(jnp.float32)
    own = [jnp.sum(query_f * key, axis=-1, keepdims=True) * SCALE for key, _ in tokens]
    peak = top
    for score in own:
        peak = jnp.maximum(peak, score)
    shrink = jnp.exp(top - peak)
    mixed = mixed * shrink
    total = total * shrink
    for score, (_, value) in zip(own, tokens):
        weight = jnp.exp(score - peak)
        mixed = mixed + weight * value
        total = total + weight
    return mixed / total


def step_kernel(
    hold_hbm,
    qold_hbm,
    w_hbm,
    cache_hbm,
    len_hbm,
    slot_hbm,
    slot1_hbm,
    hnew_hbm,
    qnew_hbm,
    old_ref,
    new_ref,
    served_ref,
    hbuf,
    wbuf,
    cbuf,
    sbuf,
    mbuf,
    fbuf,
    obuf,
    pbuf,
    qobuf,
    qnbuf,
    len_row,
    slot_row,
    len_cols,
    pick_old,
    pick_new,
    acc,
    slot_s,
    order_s,
    local_sem,
    xs_sem,
    xr_sem,
    gs_sem,
    gr_sem,
    cs_sem,
    cr_sem,
    ms_sem,
    mr_sem,
    ps_sem,
    pr_sem,
    near_sem,
):
    me = lax.axis_index("tp")
    x = me // NZ
    z = me % NZ
    other = 1 - x
    half = z % 2
    head = me // 2

    def on_ring(dz):
        return x * NZ + (z + dz) % NZ

    right, left, twin = on_ring(1), on_ring(NZ - 1), other * NZ + z
    barrier = pltpu.get_barrier_semaphore()
    for peer in (right, left, twin):
        pl.semaphore_signal(barrier, inc=1, device_id={"tp": peer}, device_id_type=MESH)

    loads = [
        (slot1_hbm, slot_s),
        (hold_hbm.at[x], hbuf.at[z, x, 0]),
        (hnew_hbm.at[x], hbuf.at[z, x, 1]),
        (slot_hbm, slot_row),
        (len_hbm, len_row),
        (cache_hbm, cbuf),
        (w_hbm, wbuf),
        (qold_hbm, qobuf),
        (qnew_hbm, qnbuf),
    ]
    loads = [
        pltpu.make_async_copy(src, dst, local_sem.at[i]) for i, (src, dst) in enumerate(loads)
    ]
    for c in loads:
        c.start()
    loads[0].wait()

    def find(u, carry):
        found = 0
        for r in range(32):
            found = jnp.where(slot_s[32 * half + r] == 2 * u + half, r, found)
        order_s[u] = found
        return carry

    lax.fori_loop(0, TP, find, 0)
    for c in loads[1:5]:
        c.wait()

    pl.semaphore_wait(barrier, 3)

    xcopies = []
    for p, src in enumerate((hold_hbm, hnew_hbm)):
        c = remote(src.at[other], hbuf.at[z, x, p], xs_sem.at[p], xr_sem.at[p], twin)
        c.start()
        xcopies.append(c)

    steps = ((8, 7), (7, 8))
    planes = (x, other)
    sent = []

    def ring(stream, way, k, p):
        slot = (z + (NZ - k if way == 0 else k)) % NZ
        block = hbuf.at[slot, planes[stream], p]
        where = ((stream * 2 + way) * 8 + k) * 2 + p
        return remote(block, block, gs_sem.at[where], gr_sem.at[where], right if way == 0 else left)

    def forward(stream, way, k, p):
        c = ring(stream, way, k, p)
        c.start()
        sent.append(c)

    for p in range(2):
        for way in range(2):
            forward(0, way, 0, p)

    def greet(i, dist):
        for way, dz in ((0, dist), (1, NZ - dist)):
            pl.semaphore_signal(
                near_sem.at[2 * i + way],
                inc=1,
                device_id={"tp": on_ring(dz)},
                device_id_type=MESH,
            )

    def greeted(i):
        for way in range(2):
            pl.semaphore_wait(near_sem.at[2 * i + way], 1)

    greet(0, 1)
    for p in range(2):
        xcopies[p].wait_recv()
        for way in range(2):
            forward(1, way, 0, p)
    greeted(0)
    greet(1, 2)

    acc[...] = jnp.zeros_like(acc)
    rid = lax.broadcasted_iota(jnp.int32, (TP * 8, 64), 0)
    col = lax.broadcasted_iota(jnp.int32, (TP * 8, 64), 1)
    j = rid & 7
    d = rid >> 3
    pick_old[...] = (
        (slot_row[...] == jnp.where(j < 2, 2 * d + j, -1)).astype(jnp.float32).astype(jnp.bfloat16)
    )
    pick_new[...] = (
        (col == jnp.where((j >= 2) & (j < 4), 2 * d + j - 2, -1))
        .astype(jnp.float32)
        .astype(jnp.bfloat16)
    )
    eye = lax.broadcasted_iota(jnp.int32, (64, 64), 0) == lax.broadcasted_iota(
        jnp.int32, (64, 64), 1
    )
    lengths_f = len_row[...].astype(jnp.float32)
    column = jnp.sum(jnp.where(eye, lengths_f, 0.0), axis=1, keepdims=True)
    len_cols[...] = jnp.broadcast_to(column, (64, 128))

    greeted(1)
    greet(2, 4)
    loads[5].wait()
    greeted(2)

    order = [(0, 8)]
    for dz in range(7, 0, -1):
        order += [(0, dz), (1, dz), (0, NZ - dz), (1, NZ - dz)]
    order += [(1, 0), (1, 8)]
    cache_copies = []

    def send_blocks(count):
        for _ in range(count):
            i = len(cache_copies)
            if i == len(order):
                return
            dx, dz = order[i]
            target = (x + dx) % 2 * NZ + (z + dz) % NZ
            sbuf[i] = cbuf[order_s[target]]
            c = remote(
                sbuf.at[i], served_ref.at[half, head], cs_sem.at[i], cr_sem.at[i], target
            )
            c.start()
            cache_copies.append(c)

    def multiply(stream, slot):
        plane = planes[stream]
        rows = pl.ds(pl.multiple_of((plane * NZ + slot) * 256, 256), 256)
        acc[...] += jnp.dot(
            hbuf[slot, plane].reshape(128, 256), wbuf[rows, :], preferred_element_type=jnp.float32
        )

    send_blocks(5)
    loads[6].wait()
    for k in range(8):
        for stream in range(2):
            for p in range(2):
                for way in range(2):
                    if k >= steps[stream][way]:
                        continue
                    ring(stream, way, k, p).wait_recv()
                    if k + 1 < steps[stream][way]:
                        forward(stream, way, k + 1, p)
        send_blocks(4)
        if k == 0:
            multiply(0, z)
            multiply(1, z)
        for stream in range(2):
            for way in range(2):
                if k < steps[stream][way]:
                    multiply(stream, (z + (NZ - k - 1 if way == 0 else k + 1)) % NZ)

    fresh = acc[...].astype(jnp.bfloat16)
    obuf[...] = fresh[:64].reshape(2, 32, 128)
    partner = on_ring(NZ + 1 - 2 * half)
    pcopy = remote(obuf.at[1 - half], pbuf.at[half], ps_sem, pr_sem, partner)
    pcopy.start()
    messages = jnp.dot(pick_old[...], fresh[:64], preferred_element_type=jnp.float32) + jnp.dot(
        pick_new[...], fresh[64:], preferred_element_type=jnp.float32
    )
    mbuf[...] = messages.astype(jnp.bfloat16).reshape(TP, 8, 128)
    message_copies = []
    for i in range(1, TP):
        target = (me + i) % TP
        c = remote(mbuf.at[target], fbuf.at[me], ms_sem.at[i], mr_sem.at[i], target)
        c.start()
        message_copies.append(c)
    pbuf[half] = obuf[half]
    fbuf[me] = mbuf[me]
    served_ref[half, head] = cbuf[order_s[me]]

    loads[7].wait()
    loads[8].wait()
    stored_old = []
    for c in range(2):
        entries = pl.ds(16 * c, 16)
        limit = len_cols[pl.ds(pl.multiple_of(32 * half + 16 * c, 16), 16), :][:, None, :64]
        stored_old.append(stored_part(qobuf[entries], cbuf[entries], limit))
    pcopy.wait()
    for c in range(2):
        entries = pl.ds(16 * c, 16)
        tokens = [
            (
                pbuf[0, entries].astype(jnp.float32)[:, None, :],
                pbuf[1, entries].astype(jnp.float32)[:, None, :],
            )
        ]
        old_ref[entries] = with_tokens(qobuf[entries], stored_old[c], tokens).astype(jnp.bfloat16)

    for c in cache_copies:
        c.wait()
    stored_new = []
    new_len = []
    for p in range(2):
        count = jnp.sum(
            jnp.where(slot_row[...] == 2 * me + p, lengths_f, 0.0), axis=1, keepdims=True
        )
        new_len.append(count)
        queries = qnbuf[p].reshape(16, 8, 128)
        stored_new.append(stored_part(queries, served_ref[p], count.reshape(1, 1, 1)))
    for c in message_copies:
        c.wait()
    received = fbuf[...].astype(jnp.float32).reshape(16, 2, 8, 128)
    for p in range(2):
        queries = qnbuf[p].reshape(16, 8, 128)
        first_key, first_value = received[:, 0, p : p + 1], received[:, 1, p : p + 1]
        tokens = [
            (first_key, first_value),
            (received[:, 0, p + 2 : p + 3], received[:, 1, p + 2 : p + 3]),
        ]
        attended = with_tokens(queries, stored_new[p], tokens)
        new_ref[p] = attended.astype(jnp.bfloat16).reshape(128, 128)
        row = lax.broadcasted_iota(jnp.int32, (1, 64, 256), 1).astype(jnp.float32)
        token = jnp.concatenate([first_key, first_value], axis=2)
        served_ref[p] = jnp.where(
            row == new_len[p].reshape(1, 1, 1), token, served_ref[p].astype(jnp.float32)
        ).astype(jnp.bfloat16)

    for c in sent:
        c.wait_send()
    for c in xcopies:
        c.wait_send()


def shards(hidden_old, queries_old, kv_weight, cache, lengths, slot, hidden_new, queries_new):
    any_spec = pl.BlockSpec(memory_space=pl.ANY)
    vmem = pl.BlockSpec(memory_space=pltpu.VMEM)
    dma = pltpu.SemaphoreType.DMA
    bf = jnp.bfloat16
    attended_old, attended_new, served = pl.pallas_call(
        step_kernel,
        out_shape=(
            jax.ShapeDtypeStruct((32, 8, 128), bf),
            jax.ShapeDtypeStruct((2, 128, 128), bf),
            jax.ShapeDtypeStruct((2, 16, 64, 256), bf),
        ),
        in_specs=[any_spec] * 9,
        out_specs=(vmem, vmem, vmem),
        scratch_shapes=[
            pltpu.VMEM((NZ, 2, 2, 64, 256), bf),
            pltpu.VMEM((8192, 128), bf),
            pltpu.VMEM((32, 64, 256), bf),
            pltpu.VMEM((32, 64, 256), bf),
            pltpu.VMEM((TP, 8, 128), bf),
            pltpu.VMEM((TP, 8, 128), bf),
            pltpu.VMEM((2, 32, 128), bf),
            pltpu.VMEM((2, 32, 128), bf),
            pltpu.VMEM((32, 8, 128), bf),
            pltpu.VMEM((2, 128, 128), bf),
            pltpu.VMEM((1, 64), jnp.int32),
            pltpu.VMEM((1, 64), jnp.int32),
            pltpu.VMEM((64, 128), jnp.float32),
            pltpu.VMEM((TP * 8, 64), bf),
            pltpu.VMEM((TP * 8, 64), bf),
            pltpu.VMEM((128, 128), jnp.float32),
            pltpu.SMEM((64,), jnp.int32),
            pltpu.SMEM((TP,), jnp.int32),
            dma((9,)),
            dma((2,)),
            dma((2,)),
            dma((64,)),
            dma((64,)),
            dma((31,)),
            dma((31,)),
            dma((32,)),
            dma((32,)),
            dma,
            dma,
            pltpu.SemaphoreType.REGULAR((6,)),
        ],
        compiler_params=pltpu.CompilerParams(
            collective_id=0, has_side_effects=True, vmem_limit_bytes=60 * 1024 * 1024
        ),
        cost_estimate=pl.CostEstimate(
            flops=2 * 128 * 8192 * 128, bytes_accessed=5 * 1024 * 1024, transcendentals=0
        ),
    )(
        hidden_old,
        queries_old,
        kv_weight,
        cache,
        lengths.reshape(1, 64),
        slot.reshape(1, 64),
        slot,
        hidden_new,
        queries_new,
    )
    return attended_old, attended_new, served.reshape(2, 1024, 256)


def solution(mesh):
    placed = (
        P(None, "rep", "tp"),
        P(("rep", "tp"), None, None),
        P(None, "tp"),
        P(("rep", "tp"), None, None),
        P("rep"),
        P("rep"),
        P(None, "rep", "tp"),
        P(("rep", "tp"), None, None),
    )
    return jax.shard_map(
        shards,
        mesh=mesh,
        in_specs=placed,
        out_specs=(
            P(("rep", "tp"), None, None),
            P(("rep", "tp"), None, None),
            P(("rep", "tp"), None, None),
        ),
        check_vma=False,
    )
```

```python
import jax
import jax.numpy as jnp
from jax import lax
from jax.experimental import pallas as pl
from jax.experimental.pallas import tpu as pltpu
from jax.sharding import PartitionSpec as P

MESH = pl.DeviceIdType.MESH
TP = 32
NZ = 16
SCALE = 1.0 / 128.0**0.5


def remote(src, dst, send_sem, recv_sem, target):
    return pltpu.make_async_remote_copy(
        src_ref=src,
        dst_ref=dst,
        send_sem=send_sem,
        recv_sem=recv_sem,
        device_id={"tp": target},
        device_id_type=MESH,
    )


def stored_part(queries, block, limit):
    keys = block[:, :, :128]
    values = block[:, :, 128:]
    scores = (
        jnp.einsum("egd,eld->egl", queries, keys, preferred_element_type=jnp.float32) * SCALE
    )
    position = lax.broadcasted_iota(jnp.int32, scores.shape, 2).astype(jnp.float32)
    scores = jnp.where(position < limit, scores, -jnp.inf)
    top = jnp.max(scores, axis=-1, keepdims=True)
    weights = jnp.exp(scores - top)
    total = jnp.sum(weights, axis=-1, keepdims=True)
    mixed = jnp.einsum(
        "egl,eld->egd", weights.astype(jnp.bfloat16), values, preferred_element_type=jnp.float32
    )
    return mixed, top, total


def with_tokens(queries, stored, tokens):
    mixed, top, total = stored
    query_f = queries.astype(jnp.float32)
    own = [jnp.sum(query_f * key, axis=-1, keepdims=True) * SCALE for key, _ in tokens]
    peak = top
    for score in own:
        peak = jnp.maximum(peak, score)
    shrink = jnp.exp(top - peak)
    mixed = mixed * shrink
    total = total * shrink
    for score, (_, value) in zip(own, tokens):
        weight = jnp.exp(score - peak)
        mixed = mixed + weight * value
        total = total + weight
    return mixed / total


def step_kernel(
    hold_hbm,
    qold_hbm,
    w_hbm,
    cache_hbm,
    len_hbm,
    slot_hbm,
    slot1_hbm,
    hnew_hbm,
    qnew_hbm,
    old_ref,
    new_ref,
    served_ref,
    hbuf,
    wbuf,
    cbuf,
    sbuf,
    mbuf,
    fbuf,
    obuf,
    pbuf,
    qobuf,
    qnbuf,
    len_row,
    slot_row,
    len_cols,
    pick_old,
    pick_new,
    acc,
    slot_s,
    order_s,
    local_sem,
    xs_sem,
    xr_sem,
    gs_sem,
    gr_sem,
    cs_sem,
    cr_sem,
    ms_sem,
    mr_sem,
    ps_sem,
    pr_sem,
    near_sem,
):
    me = lax.axis_index("tp")
    x = me // NZ
    z = me % NZ
    other = 1 - x
    half = z % 2
    head = me // 2

    def on_ring(dz):
        return x * NZ + (z + dz) % NZ

    right, left, twin = on_ring(1), on_ring(NZ - 1), other * NZ + z
    barrier = pltpu.get_barrier_semaphore()
    for peer in (right, left, twin):
        pl.semaphore_signal(barrier, inc=1, device_id={"tp": peer}, device_id_type=MESH)

    loads = [
        (slot1_hbm, slot_s),
        (hold_hbm.at[x], hbuf.at[z, x, 0]),
        (hnew_hbm.at[x], hbuf.at[z, x, 1]),
        (slot_hbm, slot_row),
        (len_hbm, len_row),
        (cache_hbm, cbuf),
        (w_hbm, wbuf),
        (qold_hbm, qobuf),
        (qnew_hbm, qnbuf),
    ]
    loads = [
        pltpu.make_async_copy(src, dst, local_sem.at[i]) for i, (src, dst) in enumerate(loads)
    ]
    for c in loads:
        c.start()
    loads[0].wait()

    def find(u, carry):
        found = 0
        for r in range(32):
            found = jnp.where(slot_s[32 * half + r] == 2 * u + half, r, found)
        order_s[u] = found
        return carry

    lax.fori_loop(0, TP, find, 0)
    for c in loads[1:5]:
        c.wait()

    pl.semaphore_wait(barrier, 3)

    xcopies = []
    for p, src in enumerate((hold_hbm, hnew_hbm)):
        c = remote(src.at[other], hbuf.at[z, x, p], xs_sem.at[p], xr_sem.at[p], twin)
        c.start()
        xcopies.append(c)

    steps = ((8, 7), (7, 8))
    planes = (x, other)
    sent = []

    def ring(stream, way, k, p):
        slot = (z + (NZ - k if way == 0 else k)) % NZ
        block = hbuf.at[slot, planes[stream], p]
        where = ((stream * 2 + way) * 8 + k) * 2 + p
        return remote(block, block, gs_sem.at[where], gr_sem.at[where], right if way == 0 else left)

    def forward(stream, way, k, p):
        c = ring(stream, way, k, p)
        c.start()
        sent.append(c)

    for p in range(2):
        for way in range(2):
            forward(0, way, 0, p)

    def greet(i, dist):
        for way, dz in ((0, dist), (1, NZ - dist)):
            pl.semaphore_signal(
                near_sem.at[2 * i + way],
                inc=1,
                device_id={"tp": on_ring(dz)},
                device_id_type=MESH,
            )

    def greeted(i):
        for way in range(2):
            pl.semaphore_wait(near_sem.at[2 * i + way], 1)

    greet(0, 1)
    for p in range(2):
        xcopies[p].wait_recv()
        for way in range(2):
            forward(1, way, 0, p)
    greeted(0)
    greet(1, 2)

    acc[...] = jnp.zeros_like(acc)
    rid = lax.broadcasted_iota(jnp.int32, (TP * 8, 64), 0)
    col = lax.broadcasted_iota(jnp.int32, (TP * 8, 64), 1)
    j = rid & 7
    d = rid >> 3
    pick_old[...] = (
        (slot_row[...] == jnp.where(j < 2, 2 * d + j, -1)).astype(jnp.float32).astype(jnp.bfloat16)
    )
    pick_new[...] = (
        (col == jnp.where((j >= 2) & (j < 4), 2 * d + j - 2, -1))
        .astype(jnp.float32)
        .astype(jnp.bfloat16)
    )
    eye = lax.broadcasted_iota(jnp.int32, (64, 64), 0) == lax.broadcasted_iota(
        jnp.int32, (64, 64), 1
    )
    lengths_f = len_row[...].astype(jnp.float32)
    column = jnp.sum(jnp.where(eye, lengths_f, 0.0), axis=1, keepdims=True)
    len_cols[...] = jnp.broadcast_to(column, (64, 128))

    greeted(1)
    greet(2, 4)
    loads[5].wait()
    greeted(2)

    order = [(0, 8)]
    for dz in range(7, 0, -1):
        order += [(0, dz), (1, dz), (0, NZ - dz), (1, NZ - dz)]
    order += [(1, 0), (1, 8)]
    cache_copies = []

    def send_blocks(count):
        for _ in range(count):
            i = len(cache_copies)
            if i == len(order):
                return
            dx, dz = order[i]
            target = (x + dx) % 2 * NZ + (z + dz) % NZ
            sbuf[i] = cbuf[order_s[target]]
            c = remote(
                sbuf.at[i], served_ref.at[half, head], cs_sem.at[i], cr_sem.at[i], target
            )
            c.start()
            cache_copies.append(c)

    def multiply(stream, slot):
        plane = planes[stream]
        rows = pl.ds(pl.multiple_of((plane * NZ + slot) * 256, 256), 256)
        acc[...] += jnp.dot(
            hbuf[slot, plane].reshape(128, 256), wbuf[rows, :], preferred_element_type=jnp.float32
        )

    send_blocks(5)
    loads[6].wait()
    for k in range(8):
        for stream in range(2):
            for p in range(2):
                for way in range(2):
                    if k >= steps[stream][way]:
                        continue
                    ring(stream, way, k, p).wait_recv()
                    if k + 1 < steps[stream][way]:
                        forward(stream, way, k + 1, p)
        send_blocks(4)
        if k == 0:
            multiply(0, z)
            multiply(1, z)
        for stream in range(2):
            for way in range(2):
                if k < steps[stream][way]:
                    multiply(stream, (z + (NZ - k - 1 if way == 0 else k + 1)) % NZ)

    fresh = acc[...].astype(jnp.bfloat16)
    obuf[...] = fresh[:64].reshape(2, 32, 128)
    partner = on_ring(NZ + 1 - 2 * half)
    pcopy = remote(obuf.at[1 - half], pbuf.at[half], ps_sem, pr_sem, partner)
    pcopy.start()
    messages = jnp.dot(pick_old[...], fresh[:64], preferred_element_type=jnp.float32) + jnp.dot(
        pick_new[...], fresh[64:], preferred_element_type=jnp.float32
    )
    mbuf[...] = messages.astype(jnp.bfloat16).reshape(TP, 8, 128)
    message_copies = []
    for i in range(1, TP):
        target = (me + i) % TP
        c = remote(mbuf.at[target], fbuf.at[me], ms_sem.at[i], mr_sem.at[i], target)
        c.start()
        message_copies.append(c)
    pbuf[half] = obuf[half]
    fbuf[me] = mbuf[me]
    served_ref[half, head] = cbuf[order_s[me]]

    loads[7].wait()
    loads[8].wait()
    stored_old = []
    for c in range(2):
        entries = pl.ds(16 * c, 16)
        limit = len_cols[pl.ds(pl.multiple_of(32 * half + 16 * c, 16), 16), :][:, None, :64]
        stored_old.append(stored_part(qobuf[entries], cbuf[entries], limit))
    pcopy.wait()
    for c in range(2):
        entries = pl.ds(16 * c, 16)
        tokens = [
            (
                pbuf[0, entries].astype(jnp.float32)[:, None, :],
                pbuf[1, entries].astype(jnp.float32)[:, None, :],
            )
        ]
        old_ref[entries] = with_tokens(qobuf[entries], stored_old[c], tokens).astype(jnp.bfloat16)

    for c in cache_copies:
        c.wait()
    stored_new = []
    new_len = []
    for p in range(2):
        count = jnp.sum(
            jnp.where(slot_row[...] == 2 * me + p, lengths_f, 0.0), axis=1, keepdims=True
        )
        new_len.append(count)
        queries = qnbuf[p].reshape(16, 8, 128)
        stored_new.append(stored_part(queries, served_ref[p], count.reshape(1, 1, 1)))
    for c in message_copies:
        c.wait()
    received = fbuf[...].astype(jnp.float32).reshape(16, 2, 8, 128)
    for p in range(2):
        queries = qnbuf[p].reshape(16, 8, 128)
        first_key, first_value = received[:, 0, p : p + 1], received[:, 1, p : p + 1]
        tokens = [
            (first_key, first_value),
            (received[:, 0, p + 2 : p + 3], received[:, 1, p + 2 : p + 3]),
        ]
        attended = with_tokens(queries, stored_new[p], tokens)
        new_ref[p] = attended.astype(jnp.bfloat16).reshape(128, 128)
        row = lax.broadcasted_iota(jnp.int32, (1, 64, 256), 1).astype(jnp.float32)
        token = jnp.concatenate([first_key, first_value], axis=2)
        served_ref[p] = jnp.where(
            row == new_len[p].reshape(1, 1, 1), token, served_ref[p].astype(jnp.float32)
        ).astype(jnp.bfloat16)

    for c in sent:
        c.wait_send()
    for c in xcopies:
        c.wait_send()


def hand_over(old_in, new_in, served_in, old_ref, new_ref, served_ref, sem):
    copies = [
        pltpu.make_async_copy(served_in, served_ref, sem.at[0]),
        pltpu.make_async_copy(old_in, old_ref, sem.at[1]),
        pltpu.make_async_copy(new_in, new_ref, sem.at[2]),
    ]
    for c in copies:
        c.start()
    for c in copies:
        c.wait()


def shards(hidden_old, queries_old, kv_weight, cache, lengths, slot, hidden_new, queries_new):
    hbm = pl.BlockSpec(memory_space=pltpu.HBM)
    any_spec = pl.BlockSpec(memory_space=pl.ANY)
    vmem = pl.BlockSpec(memory_space=pltpu.VMEM)
    dma = pltpu.SemaphoreType.DMA
    bf = jnp.bfloat16
    parts = pl.pallas_call(
        step_kernel,
        out_shape=(
            jax.ShapeDtypeStruct((32, 8, 128), bf),
            jax.ShapeDtypeStruct((2, 128, 128), bf),
            jax.ShapeDtypeStruct((2, 16, 64, 256), bf),
        ),
        in_specs=[hbm] * 9,
        out_specs=(vmem, vmem, vmem),
        scratch_shapes=[
            pltpu.VMEM((NZ, 2, 2, 64, 256), bf),
            pltpu.VMEM((8192, 128), bf),
            pltpu.VMEM((32, 64, 256), bf),
            pltpu.VMEM((32, 64, 256), bf),
            pltpu.VMEM((TP, 8, 128), bf),
            pltpu.VMEM((TP, 8, 128), bf),
            pltpu.VMEM((2, 32, 128), bf),
            pltpu.VMEM((2, 32, 128), bf),
            pltpu.VMEM((32, 8, 128), bf),
            pltpu.VMEM((2, 128, 128), bf),
            pltpu.VMEM((1, 64), jnp.int32),
            pltpu.VMEM((1, 64), jnp.int32),
            pltpu.VMEM((64, 128), jnp.float32),
            pltpu.VMEM((TP * 8, 64), bf),
            pltpu.VMEM((TP * 8, 64), bf),
            pltpu.VMEM((128, 128), jnp.float32),
            pltpu.SMEM((64,), jnp.int32),
            pltpu.SMEM((TP,), jnp.int32),
            dma((9,)),
            dma((2,)),
            dma((2,)),
            dma((64,)),
            dma((64,)),
            dma((31,)),
            dma((31,)),
            dma((32,)),
            dma((32,)),
            dma,
            dma,
            pltpu.SemaphoreType.REGULAR((6,)),
        ],
        compiler_params=pltpu.CompilerParams(
            collective_id=0, has_side_effects=True, vmem_limit_bytes=24 * 1024 * 1024
        ),
        cost_estimate=pl.CostEstimate(
            flops=2 * 128 * 8192 * 128, bytes_accessed=5 * 1024 * 1024, transcendentals=0
        ),
    )(
        *(
            pltpu.with_memory_space_constraint(array, pltpu.HBM)
            for array in (
                hidden_old,
                queries_old,
                kv_weight,
                cache,
                lengths.reshape(1, 64),
                slot.reshape(1, 64),
                slot,
                hidden_new,
                queries_new,
            )
        )
    )
    attended_old, attended_new, served = pl.pallas_call(
        hand_over,
        out_shape=tuple(jax.ShapeDtypeStruct(part.shape, part.dtype) for part in parts),
        in_specs=[any_spec] * 3,
        out_specs=(any_spec,) * 3,
        scratch_shapes=[dma((3,))],
        compiler_params=pltpu.CompilerParams(vmem_limit_bytes=16 * 1024 * 1024),
        cost_estimate=pl.CostEstimate(flops=0, bytes_accessed=2400000, transcendentals=0),
    )(*parts)
    return attended_old, attended_new, served.reshape(2, 1024, 256)


def solution(mesh):
    placed = (
        P(None, "rep", "tp"),
        P(("rep", "tp"), None, None),
        P(None, "tp"),
        P(("rep", "tp"), None, None),
        P("rep"),
        P("rep"),
        P(None, "rep", "tp"),
        P(("rep", "tp"), None, None),
    )
    return jax.shard_map(
        shards,
        mesh=mesh,
        in_specs=placed,
        out_specs=(
            P(("rep", "tp"), None, None),
            P(("rep", "tp"), None, None),
            P(("rep", "tp"), None, None),
        ),
        check_vma=False,
    )
```

```python
import jax
import jax.numpy as jnp
from jax import lax
from jax.experimental import pallas as pl
from jax.experimental.pallas import tpu as pltpu
from jax.sharding import PartitionSpec as P

MESH = pl.DeviceIdType.MESH
TP = 32
NZ = 16
SCALE = 1.0 / 128.0**0.5


def remote(src, dst, send_sem, recv_sem, target):
    return pltpu.make_async_remote_copy(
        src_ref=src,
        dst_ref=dst,
        send_sem=send_sem,
        recv_sem=recv_sem,
        device_id={"tp": target},
        device_id_type=MESH,
    )


def stored_part(queries, block, limit):
    keys = block[:, :, :128]
    values = block[:, :, 128:]
    scores = (
        jnp.einsum("egd,eld->egl", queries, keys, preferred_element_type=jnp.float32) * SCALE
    )
    position = lax.broadcasted_iota(jnp.int32, scores.shape, 2).astype(jnp.float32)
    scores = jnp.where(position < limit, scores, -jnp.inf)
    top = jnp.max(scores, axis=-1, keepdims=True)
    weights = jnp.exp(scores - top)
    total = jnp.sum(weights, axis=-1, keepdims=True)
    mixed = jnp.einsum(
        "egl,eld->egd", weights.astype(jnp.bfloat16), values, preferred_element_type=jnp.float32
    )
    return mixed, top, total


def with_tokens(queries, stored, tokens):
    mixed, top, total = stored
    query_f = queries.astype(jnp.float32)
    own = [jnp.sum(query_f * key, axis=-1, keepdims=True) * SCALE for key, _ in tokens]
    peak = top
    for score in own:
        peak = jnp.maximum(peak, score)
    shrink = jnp.exp(top - peak)
    mixed = mixed * shrink
    total = total * shrink
    for score, (_, value) in zip(own, tokens):
        weight = jnp.exp(score - peak)
        mixed = mixed + weight * value
        total = total + weight
    return mixed / total


def step_kernel(
    hold_hbm,
    qold_hbm,
    w_hbm,
    cache_hbm,
    len_hbm,
    slot_hbm,
    slot1_hbm,
    hnew_hbm,
    qnew_hbm,
    old_ref,
    new_ref,
    served_ref,
    hbuf,
    wbuf,
    cbuf,
    sbuf,
    mbuf,
    fbuf,
    obuf,
    pbuf,
    qobuf,
    qnbuf,
    len_row,
    slot_row,
    len_cols,
    pick_old,
    pick_new,
    acc,
    mixed_buf,
    top_buf,
    total_buf,
    slot_s,
    order_s,
    local_sem,
    xs_sem,
    xr_sem,
    gs_sem,
    gr_sem,
    cs_sem,
    cr_sem,
    ms_sem,
    mr_sem,
    ps_sem,
    pr_sem,
    near_sem,
):
    me = lax.axis_index("tp")
    x = me // NZ
    z = me % NZ
    other = 1 - x
    half = z % 2
    head = me // 2

    def on_ring(dz):
        return x * NZ + (z + dz) % NZ

    right, left, twin = on_ring(1), on_ring(NZ - 1), other * NZ + z
    barrier = pltpu.get_barrier_semaphore()
    for peer in (right, left, twin):
        pl.semaphore_signal(barrier, inc=1, device_id={"tp": peer}, device_id_type=MESH)

    loads = [
        (slot1_hbm, slot_s),
        (hold_hbm.at[x], hbuf.at[z, x, 0]),
        (hnew_hbm.at[x], hbuf.at[z, x, 1]),
        (slot_hbm, slot_row),
        (len_hbm, len_row),
        (cache_hbm, cbuf),
        (w_hbm, wbuf),
        (qold_hbm, qobuf),
        (qnew_hbm, qnbuf),
    ]
    loads = [
        pltpu.make_async_copy(src, dst, local_sem.at[i]) for i, (src, dst) in enumerate(loads)
    ]
    for c in loads:
        c.start()
    for c in loads[1:3]:
        c.wait()

    pl.semaphore_wait(barrier, 3)

    xcopies = []
    for p, src in enumerate((hold_hbm, hnew_hbm)):
        c = remote(src.at[other], hbuf.at[z, x, p], xs_sem.at[p], xr_sem.at[p], twin)
        c.start()
        xcopies.append(c)

    steps = ((8, 7), (7, 8))
    planes = (x, other)
    sent = []

    def ring(stream, way, k, p):
        slot = (z + (NZ - k if way == 0 else k)) % NZ
        block = hbuf.at[slot, planes[stream], p]
        where = ((stream * 2 + way) * 8 + k) * 2 + p
        return remote(block, block, gs_sem.at[where], gr_sem.at[where], right if way == 0 else left)

    def forward(stream, way, k, p):
        c = ring(stream, way, k, p)
        c.start()
        sent.append(c)

    for p in range(2):
        for way in range(2):
            forward(0, way, 0, p)

    def greet(i, dist):
        for way, dz in ((0, dist), (1, NZ - dist)):
            pl.semaphore_signal(
                near_sem.at[2 * i + way],
                inc=1,
                device_id={"tp": on_ring(dz)},
                device_id_type=MESH,
            )

    def greeted(i):
        for way in range(2):
            pl.semaphore_wait(near_sem.at[2 * i + way], 1)

    loads[0].wait()

    def find(u, carry):
        found = 0
        for r in range(32):
            found = jnp.where(slot_s[32 * half + r] == 2 * u + half, r, found)
        order_s[u] = found
        return carry

    lax.fori_loop(0, TP, find, 0)
    for c in loads[3:5]:
        c.wait()
    for p in range(2):
        xcopies[p].wait_recv()
        for way in range(2):
            forward(1, way, 0, p)

    acc[...] = jnp.zeros_like(acc)
    rid = lax.broadcasted_iota(jnp.int32, (TP * 8, 64), 0)
    col = lax.broadcasted_iota(jnp.int32, (TP * 8, 64), 1)
    j = rid & 7
    d = rid >> 3
    pick_old[...] = (
        (slot_row[...] == jnp.where(j < 2, 2 * d + j, -1)).astype(jnp.float32).astype(jnp.bfloat16)
    )
    pick_new[...] = (
        (col == jnp.where((j >= 2) & (j < 4), 2 * d + j - 2, -1))
        .astype(jnp.float32)
        .astype(jnp.bfloat16)
    )
    eye = lax.broadcasted_iota(jnp.int32, (64, 64), 0) == lax.broadcasted_iota(
        jnp.int32, (64, 64), 1
    )
    lengths_f = len_row[...].astype(jnp.float32)
    column = jnp.sum(jnp.where(eye, lengths_f, 0.0), axis=1, keepdims=True)
    len_cols[...] = jnp.broadcast_to(column, (64, 128))

    loads[5].wait()

    order = [(0, 8)]
    for dz in range(7, 0, -1):
        order += [(0, dz), (1, dz), (0, NZ - dz), (1, NZ - dz)]
    order += [(1, 0), (1, 8)]
    cache_copies = []

    def send_blocks(count):
        for _ in range(count):
            i = len(cache_copies)
            if i == len(order):
                return
            dx, dz = order[i]
            target = (x + dx) % 2 * NZ + (z + dz) % NZ
            sbuf[i] = cbuf[order_s[target]]
            c = remote(
                sbuf.at[i], served_ref.at[half, head], cs_sem.at[i], cr_sem.at[i], target
            )
            c.start()
            cache_copies.append(c)

    def multiply(stream, slot):
        plane = planes[stream]
        rows = pl.ds(pl.multiple_of((plane * NZ + slot) * 256, 256), 256)
        acc[...] += jnp.dot(
            hbuf[slot, plane].reshape(128, 256), wbuf[rows, :], preferred_element_type=jnp.float32
        )

    loads[6].wait()
    for k in range(8):
        for stream in range(2):
            for p in range(2):
                for way in range(2):
                    if k >= steps[stream][way]:
                        continue
                    ring(stream, way, k, p).wait_recv()
                    if k + 1 < steps[stream][way]:
                        forward(stream, way, k + 1, p)
        if k == 0:
            greet(0, 2)
        elif k == 1:
            greeted(0)
            greet(1, 4)
        elif k == 2:
            greeted(1)
        send_blocks((0, 0, 5, 3, 3, 3, 3, 3)[k])
        if k == 0:
            multiply(0, z)
            multiply(1, z)
        for stream in range(2):
            for way in range(2):
                if k < steps[stream][way]:
                    multiply(stream, (z + (NZ - k - 1 if way == 0 else k + 1)) % NZ)

    fresh = acc[...].astype(jnp.bfloat16)
    obuf[...] = fresh[:64].reshape(2, 32, 128)
    partner = on_ring(NZ + 1 - 2 * half)
    pcopy = remote(obuf.at[1 - half], pbuf.at[half], ps_sem, pr_sem, partner)
    pcopy.start()
    messages = jnp.dot(pick_old[...], fresh[:64], preferred_element_type=jnp.float32) + jnp.dot(
        pick_new[...], fresh[64:], preferred_element_type=jnp.float32
    )
    mbuf[...] = messages.astype(jnp.bfloat16).reshape(TP, 8, 128)
    message_copies = []
    for i in range(1, TP):
        target = (me + i) % TP
        c = remote(mbuf.at[target], fbuf.at[me], ms_sem.at[i], mr_sem.at[i], target)
        c.start()
        message_copies.append(c)
    send_blocks(31)
    pbuf[half] = obuf[half]
    fbuf[me] = mbuf[me]
    served_ref[half, head] = cbuf[order_s[me]]

    loads[7].wait()
    loads[8].wait()
    stored_old = []
    for c in range(2):
        entries = pl.ds(16 * c, 16)
        limit = len_cols[pl.ds(pl.multiple_of(32 * half + 16 * c, 16), 16), :][:, None, :64]
        stored_old.append(stored_part(qobuf[entries], cbuf[entries], limit))
    pcopy.wait()
    for c in range(2):
        entries = pl.ds(16 * c, 16)
        tokens = [
            (
                pbuf[0, entries].astype(jnp.float32)[:, None, :],
                pbuf[1, entries].astype(jnp.float32)[:, None, :],
            )
        ]
        old_ref[entries] = with_tokens(qobuf[entries], stored_old[c], tokens).astype(jnp.bfloat16)

    new_len = []
    for p in range(2):
        count = jnp.sum(
            jnp.where(slot_row[...] == 2 * me + p, lengths_f, 0.0), axis=1, keepdims=True
        )
        new_len.append(count.reshape(1, 1, 1))

    def arrived(group):
        places = []
        for i in group:
            if i < len(order):
                cache_copies[i].wait_recv()
                dx, dz = order[i]
                zs = (z + NZ - dz) % NZ
                places.append((zs % 2, ((x + dx) % 2 * NZ + zs) // 2))
            else:
                places.append((half, head))
        queries = jnp.stack(
            [qnbuf[h, a] for h, a in places]
        )
        blocks = jnp.stack([served_ref[h, a] for h, a in places])
        limit = jnp.concatenate(
            [jnp.where(h == 0, new_len[0], new_len[1]) for h, _ in places], axis=0
        )
        mixed, top, total = stored_part(queries, blocks, limit)
        for n, (h, a) in enumerate(places):
            mixed_buf[h, a] = mixed[n]
            top_buf[h, a] = jnp.broadcast_to(top[n], (8, 128))
            total_buf[h, a] = jnp.broadcast_to(total[n], (8, 128))

    for g in range(4):
        arrived(range(8 * g, 8 * g + 8))
    for c in message_copies:
        c.wait()
    received = fbuf[...].astype(jnp.float32).reshape(16, 2, 8, 128)
    for p in range(2):
        queries = qnbuf[p]
        first_key, first_value = received[:, 0, p : p + 1], received[:, 1, p : p + 1]
        tokens = [
            (first_key, first_value),
            (received[:, 0, p + 2 : p + 3], received[:, 1, p + 2 : p + 3]),
        ]
        stored = (mixed_buf[p], top_buf[p][:, :, :1], total_buf[p][:, :, :1])
        attended = with_tokens(queries, stored, tokens)
        new_ref[p] = attended.astype(jnp.bfloat16).reshape(128, 128)
        row = lax.broadcasted_iota(jnp.int32, (1, 64, 256), 1).astype(jnp.float32)
        token = jnp.concatenate([first_key, first_value], axis=2)
        served_ref[p] = jnp.where(
            row == new_len[p], token, served_ref[p].astype(jnp.float32)
        ).astype(jnp.bfloat16)

    for c in cache_copies:
        c.wait_send()
    for c in sent:
        c.wait_send()
    for c in xcopies:
        c.wait_send()


def hand_over(old_in, new_in, served_in, old_ref, new_ref, served_ref, sem):
    copies = [
        pltpu.make_async_copy(served_in, served_ref, sem.at[0]),
        pltpu.make_async_copy(old_in, old_ref, sem.at[1]),
        pltpu.make_async_copy(new_in, new_ref, sem.at[2]),
    ]
    for c in copies:
        c.start()
    for c in copies:
        c.wait()


def shards(hidden_old, queries_old, kv_weight, cache, lengths, slot, hidden_new, queries_new):
    hbm = pl.BlockSpec(memory_space=pltpu.HBM)
    any_spec = pl.BlockSpec(memory_space=pl.ANY)
    vmem = pl.BlockSpec(memory_space=pltpu.VMEM)
    dma = pltpu.SemaphoreType.DMA
    bf = jnp.bfloat16
    parts = pl.pallas_call(
        step_kernel,
        out_shape=(
            jax.ShapeDtypeStruct((32, 8, 128), bf),
            jax.ShapeDtypeStruct((2, 128, 128), bf),
            jax.ShapeDtypeStruct((2, 16, 64, 256), bf),
        ),
        in_specs=[hbm] * 9,
        out_specs=(vmem, vmem, vmem),
        scratch_shapes=[
            pltpu.VMEM((NZ, 2, 2, 64, 256), bf),
            pltpu.VMEM((8192, 128), bf),
            pltpu.VMEM((32, 64, 256), bf),
            pltpu.VMEM((32, 64, 256), bf),
            pltpu.VMEM((TP, 8, 128), bf),
            pltpu.VMEM((TP, 8, 128), bf),
            pltpu.VMEM((2, 32, 128), bf),
            pltpu.VMEM((2, 32, 128), bf),
            pltpu.VMEM((32, 8, 128), bf),
            pltpu.VMEM((2, 16, 8, 128), bf),
            pltpu.VMEM((1, 64), jnp.int32),
            pltpu.VMEM((1, 64), jnp.int32),
            pltpu.VMEM((64, 128), jnp.float32),
            pltpu.VMEM((TP * 8, 64), bf),
            pltpu.VMEM((TP * 8, 64), bf),
            pltpu.VMEM((128, 128), jnp.float32),
            pltpu.VMEM((2, 16, 8, 128), jnp.float32),
            pltpu.VMEM((2, 16, 8, 128), jnp.float32),
            pltpu.VMEM((2, 16, 8, 128), jnp.float32),
            pltpu.SMEM((64,), jnp.int32),
            pltpu.SMEM((TP,), jnp.int32),
            dma((9,)),
            dma((2,)),
            dma((2,)),
            dma((64,)),
            dma((64,)),
            dma((31,)),
            dma((31,)),
            dma((32,)),
            dma((32,)),
            dma,
            dma,
            pltpu.SemaphoreType.REGULAR((4,)),
        ],
        compiler_params=pltpu.CompilerParams(
            collective_id=0, has_side_effects=True, vmem_limit_bytes=24 * 1024 * 1024
        ),
        cost_estimate=pl.CostEstimate(
            flops=2 * 128 * 8192 * 128, bytes_accessed=5 * 1024 * 1024, transcendentals=0
        ),
    )(
        *(
            pltpu.with_memory_space_constraint(array, pltpu.HBM)
            for array in (
                hidden_old,
                queries_old,
                kv_weight,
                cache,
                lengths.reshape(1, 64),
                slot.reshape(1, 64),
                slot,
                hidden_new,
                queries_new.reshape(2, 16, 8, 128),
            )
        )
    )
    attended_old, attended_new, served = pl.pallas_call(
        hand_over,
        out_shape=tuple(jax.ShapeDtypeStruct(part.shape, part.dtype) for part in parts),
        in_specs=[any_spec] * 3,
        out_specs=(any_spec,) * 3,
        scratch_shapes=[dma((3,))],
        compiler_params=pltpu.CompilerParams(vmem_limit_bytes=16 * 1024 * 1024),
        cost_estimate=pl.CostEstimate(flops=0, bytes_accessed=2400000, transcendentals=0),
    )(*parts)
    return attended_old, attended_new, served.reshape(2, 1024, 256)


def solution(mesh):
    placed = (
        P(None, "rep", "tp"),
        P(("rep", "tp"), None, None),
        P(None, "tp"),
        P(("rep", "tp"), None, None),
        P("rep"),
        P("rep"),
        P(None, "rep", "tp"),
        P(("rep", "tp"), None, None),
    )
    return jax.shard_map(
        shards,
        mesh=mesh,
        in_specs=placed,
        out_specs=(
            P(("rep", "tp"), None, None),
            P(("rep", "tp"), None, None),
            P(("rep", "tp"), None, None),
        ),
        check_vma=False,
    )
```

```python
import jax
import jax.numpy as jnp
from jax import lax
from jax.experimental import pallas as pl
from jax.experimental.pallas import tpu as pltpu
from jax.sharding import PartitionSpec as P

MESH = pl.DeviceIdType.MESH
TP = 32
NZ = 16
SCALE = 1.0 / 128.0**0.5


def remote(src, dst, send_sem, recv_sem, target):
    return pltpu.make_async_remote_copy(
        src_ref=src,
        dst_ref=dst,
        send_sem=send_sem,
        recv_sem=recv_sem,
        device_id={"tp": target},
        device_id_type=MESH,
    )


def stored_part(queries, block, limit):
    keys = block[:, :, :128]
    values = block[:, :, 128:]
    scores = (
        jnp.einsum("egd,eld->egl", queries, keys, preferred_element_type=jnp.float32) * SCALE
    )
    position = lax.broadcasted_iota(jnp.int32, scores.shape, 2).astype(jnp.float32)
    scores = jnp.where(position < limit, scores, -jnp.inf)
    top = jnp.max(scores, axis=-1, keepdims=True)
    weights = jnp.exp(scores - top)
    total = jnp.sum(weights, axis=-1, keepdims=True)
    mixed = jnp.einsum(
        "egl,eld->egd", weights.astype(jnp.bfloat16), values, preferred_element_type=jnp.float32
    )
    return mixed, top, total


def with_tokens(queries, stored, tokens):
    mixed, top, total = stored
    query_f = queries.astype(jnp.float32)
    own = [jnp.sum(query_f * key, axis=-1, keepdims=True) * SCALE for key, _ in tokens]
    peak = top
    for score in own:
        peak = jnp.maximum(peak, score)
    shrink = jnp.exp(top - peak)
    mixed = mixed * shrink
    total = total * shrink
    for score, (_, value) in zip(own, tokens):
        weight = jnp.exp(score - peak)
        mixed = mixed + weight * value
        total = total + weight
    return mixed / total


def step_kernel(
    hold_hbm,
    qold_hbm,
    w_hbm,
    cache_hbm,
    len_hbm,
    slot_hbm,
    slot1_hbm,
    hnew_hbm,
    qnew_hbm,
    old_ref,
    new_ref,
    served_ref,
    hbuf,
    wbuf,
    cbuf,
    sbuf,
    mbuf,
    fbuf,
    obuf,
    pbuf,
    qobuf,
    qnbuf,
    len_row,
    slot_row,
    len_cols,
    pick_old,
    pick_new,
    acc,
    mixed_buf,
    top_buf,
    total_buf,
    slot_s,
    order_s,
    local_sem,
    xs_sem,
    xr_sem,
    gs_sem,
    gr_sem,
    cs_sem,
    cr_sem,
    ms_sem,
    mr_sem,
    ps_sem,
    pr_sem,
    ys_sem,
    yr_sem,
    near_sem,
):
    me = lax.axis_index("tp")
    x = me // NZ
    z = me % NZ
    other = 1 - x
    half = z % 2
    head = me // 2

    def on_ring(dz):
        return x * NZ + (z + dz) % NZ

    right, left, twin = on_ring(1), on_ring(NZ - 1), other * NZ + z
    barrier = pltpu.get_barrier_semaphore()
    for peer in (right, left, twin):
        pl.semaphore_signal(barrier, inc=1, device_id={"tp": peer}, device_id_type=MESH)

    loads = [
        (slot1_hbm, slot_s),
        (hold_hbm.at[x], hbuf.at[z, x, 0]),
        (hnew_hbm.at[x], hbuf.at[z, x, 1]),
        (slot_hbm, slot_row),
        (len_hbm, len_row),
        (cache_hbm, cbuf),
        (w_hbm, wbuf),
        (qold_hbm, qobuf),
        (qnew_hbm, qnbuf),
    ]
    loads = [
        pltpu.make_async_copy(src, dst, local_sem.at[i]) for i, (src, dst) in enumerate(loads)
    ]
    for c in loads:
        c.start()
    for c in loads[1:3]:
        c.wait()

    pl.semaphore_wait(barrier, 3)

    xcopies = []
    for p, src in enumerate((hold_hbm, hnew_hbm)):
        c = remote(src.at[other], hbuf.at[z, x, p], xs_sem.at[p], xr_sem.at[p], twin)
        c.start()
        xcopies.append(c)

    steps = ((8, 7), (7, 8))
    planes = (x, other)
    sent = []

    def ring(stream, way, k, p):
        slot = (z + (NZ - k if way == 0 else k)) % NZ
        block = hbuf.at[slot, planes[stream], p]
        where = ((stream * 2 + way) * 8 + k) * 2 + p
        return remote(block, block, gs_sem.at[where], gr_sem.at[where], right if way == 0 else left)

    def forward(stream, way, k, p):
        c = ring(stream, way, k, p)
        c.start()
        sent.append(c)

    for p in range(2):
        for way in range(2):
            forward(0, way, 0, p)

    def greet(i, dist):
        for way, dz in ((0, dist), (1, NZ - dist)):
            pl.semaphore_signal(
                near_sem.at[2 * i + way],
                inc=1,
                device_id={"tp": on_ring(dz)},
                device_id_type=MESH,
            )

    def greeted(i):
        for way in range(2):
            pl.semaphore_wait(near_sem.at[2 * i + way], 1)

    loads[0].wait()

    def find(u, carry):
        found = 0
        for r in range(32):
            found = jnp.where(slot_s[32 * half + r] == 2 * u + half, r, found)
        order_s[u] = found
        return carry

    lax.fori_loop(0, TP, find, 0)
    for c in loads[3:5]:
        c.wait()
    for p in range(2):
        xcopies[p].wait_recv()
        for way in range(2):
            forward(1, way, 0, p)

    acc[...] = jnp.zeros_like(acc)
    rid = lax.broadcasted_iota(jnp.int32, (NZ * 8, 64), 0)
    col = lax.broadcasted_iota(jnp.int32, (NZ * 8, 64), 1)
    j = rid & 3
    plane = jnp.where((rid & 7) < 4, x, other)
    row = 2 * (plane * NZ + (rid >> 3)) + (j & 1)
    pick_old[...] = (
        (slot_row[...] == jnp.where(j < 2, row, -1)).astype(jnp.float32).astype(jnp.bfloat16)
    )
    pick_new[...] = (col == jnp.where(j < 2, -1, row)).astype(jnp.float32).astype(jnp.bfloat16)
    eye = lax.broadcasted_iota(jnp.int32, (64, 64), 0) == lax.broadcasted_iota(
        jnp.int32, (64, 64), 1
    )
    lengths_f = len_row[...].astype(jnp.float32)
    column = jnp.sum(jnp.where(eye, lengths_f, 0.0), axis=1, keepdims=True)
    len_cols[...] = jnp.broadcast_to(column, (64, 128))

    loads[5].wait()

    order = [(0, 8)]
    for dz in range(7, 0, -1):
        order += [(0, dz), (1, dz), (0, NZ - dz), (1, NZ - dz)]
    order += [(1, 0), (1, 8)]
    cache_copies = []

    def send_blocks(count):
        for _ in range(count):
            i = len(cache_copies)
            if i == len(order):
                return
            dx, dz = order[i]
            target = (x + dx) % 2 * NZ + (z + dz) % NZ
            sbuf[i] = cbuf[order_s[target]]
            c = remote(
                sbuf.at[i], served_ref.at[half, head], cs_sem.at[i], cr_sem.at[i], target
            )
            c.start()
            cache_copies.append(c)

    def multiply(stream, slot):
        plane = planes[stream]
        rows = pl.ds(pl.multiple_of((plane * NZ + slot) * 256, 256), 256)
        acc[...] += jnp.dot(
            hbuf[slot, plane].reshape(128, 256), wbuf[rows, :], preferred_element_type=jnp.float32
        )

    loads[6].wait()
    for k in range(8):
        for stream in range(2):
            for p in range(2):
                for way in range(2):
                    if k >= steps[stream][way]:
                        continue
                    ring(stream, way, k, p).wait_recv()
                    if k + 1 < steps[stream][way]:
                        forward(stream, way, k + 1, p)
        if k == 0:
            greet(0, 2)
        elif k == 1:
            greeted(0)
            greet(1, 4)
        elif k == 2:
            greeted(1)
        send_blocks((0, 0, 5, 3, 3, 3, 3, 3)[k])
        if k == 0:
            multiply(0, z)
            multiply(1, z)
        for stream in range(2):
            for way in range(2):
                if k < steps[stream][way]:
                    multiply(stream, (z + (NZ - k - 1 if way == 0 else k + 1)) % NZ)

    fresh = acc[...].astype(jnp.bfloat16)
    obuf[...] = fresh[:64].reshape(2, 32, 128)
    partner = on_ring(NZ + 1 - 2 * half)
    pcopy = remote(obuf.at[1 - half], pbuf.at[half], ps_sem, pr_sem, partner)
    pcopy.start()
    messages = jnp.dot(pick_old[...], fresh[:64], preferred_element_type=jnp.float32) + jnp.dot(
        pick_new[...], fresh[64:], preferred_element_type=jnp.float32
    )
    mbuf[...] = messages.astype(jnp.bfloat16).reshape(NZ, 8, 128)
    message_copies = []
    for i, dz in enumerate((8, 7, 9, 6, 10, 5, 11, 4, 12, 3, 13, 2, 14, 1, 15)):
        c = remote(
            mbuf.at[(z + dz) % NZ], fbuf.at[me], ms_sem.at[i], mr_sem.at[i], on_ring(dz)
        )
        c.start()
        message_copies.append(c)
    send_blocks(31)
    pbuf[half] = obuf[half]
    fbuf[me] = mbuf[z]
    served_ref[half, head] = cbuf[order_s[me]]

    loads[7].wait()
    loads[8].wait()
    stored_old = []
    for c in range(2):
        entries = pl.ds(16 * c, 16)
        limit = len_cols[pl.ds(pl.multiple_of(32 * half + 16 * c, 16), 16), :][:, None, :64]
        stored_old.append(stored_part(qobuf[entries], cbuf[entries], limit))
    pcopy.wait()
    for c in range(2):
        entries = pl.ds(16 * c, 16)
        tokens = [
            (
                pbuf[0, entries].astype(jnp.float32)[:, None, :],
                pbuf[1, entries].astype(jnp.float32)[:, None, :],
            )
        ]
        old_ref[entries] = with_tokens(qobuf[entries], stored_old[c], tokens).astype(jnp.bfloat16)

    for c in message_copies:
        c.wait()
    ring_rows = fbuf.at[pl.ds(pl.multiple_of(x * NZ, NZ), NZ)]
    relay = remote(ring_rows, ring_rows, ys_sem, yr_sem, twin)
    relay.start()
    new_len = []
    for p in range(2):
        count = jnp.sum(
            jnp.where(slot_row[...] == 2 * me + p, lengths_f, 0.0), axis=1, keepdims=True
        )
        new_len.append(count.reshape(1, 1, 1))

    def arrived(group):
        places = []
        for i in group:
            if i < len(order):
                cache_copies[i].wait_recv()
                dx, dz = order[i]
                zs = (z + NZ - dz) % NZ
                places.append((zs % 2, ((x + dx) % 2 * NZ + zs) // 2))
            else:
                places.append((half, head))
        queries = jnp.stack(
            [qnbuf[h, a] for h, a in places]
        )
        blocks = jnp.stack([served_ref[h, a] for h, a in places])
        limit = jnp.concatenate(
            [jnp.where(h == 0, new_len[0], new_len[1]) for h, _ in places], axis=0
        )
        mixed, top, total = stored_part(queries, blocks, limit)
        for n, (h, a) in enumerate(places):
            mixed_buf[h, a] = mixed[n]
            top_buf[h, a] = jnp.broadcast_to(top[n], (8, 128))
            total_buf[h, a] = jnp.broadcast_to(total[n], (8, 128))

    for g in range(4):
        arrived(range(8 * g, 8 * g + 8))
    relay.wait()
    received = fbuf[...].astype(jnp.float32).reshape(16, 2, 8, 128)
    mine = (lax.broadcasted_iota(jnp.int32, (16, 1, 128), 0) >> 3) == x

    def token_row(kind, j):
        return jnp.where(mine, received[:, kind, j : j + 1], received[:, kind, j + 4 : j + 5])

    for p in range(2):
        queries = qnbuf[p]
        first_key, first_value = token_row(0, p), token_row(1, p)
        tokens = [(first_key, first_value), (token_row(0, p + 2), token_row(1, p + 2))]
        stored = (mixed_buf[p], top_buf[p][:, :, :1], total_buf[p][:, :, :1])
        attended = with_tokens(queries, stored, tokens)
        new_ref[p] = attended.astype(jnp.bfloat16).reshape(128, 128)
        row = lax.broadcasted_iota(jnp.int32, (1, 64, 256), 1).astype(jnp.float32)
        token = jnp.concatenate([first_key, first_value], axis=2)
        served_ref[p] = jnp.where(
            row == new_len[p], token, served_ref[p].astype(jnp.float32)
        ).astype(jnp.bfloat16)

    for c in cache_copies:
        c.wait_send()
    for c in sent:
        c.wait_send()
    for c in xcopies:
        c.wait_send()


def hand_over(old_in, new_in, served_in, old_ref, new_ref, served_ref, sem):
    copies = [
        pltpu.make_async_copy(served_in, served_ref, sem.at[0]),
        pltpu.make_async_copy(old_in, old_ref, sem.at[1]),
        pltpu.make_async_copy(new_in, new_ref, sem.at[2]),
    ]
    for c in copies:
        c.start()
    for c in copies:
        c.wait()


def shards(hidden_old, queries_old, kv_weight, cache, lengths, slot, hidden_new, queries_new):
    hbm = pl.BlockSpec(memory_space=pltpu.HBM)
    any_spec = pl.BlockSpec(memory_space=pl.ANY)
    vmem = pl.BlockSpec(memory_space=pltpu.VMEM)
    dma = pltpu.SemaphoreType.DMA
    bf = jnp.bfloat16
    parts = pl.pallas_call(
        step_kernel,
        out_shape=(
            jax.ShapeDtypeStruct((32, 8, 128), bf),
            jax.ShapeDtypeStruct((2, 128, 128), bf),
            jax.ShapeDtypeStruct((2, 16, 64, 256), bf),
        ),
        in_specs=[hbm] * 9,
        out_specs=(vmem, vmem, vmem),
        scratch_shapes=[
            pltpu.VMEM((NZ, 2, 2, 64, 256), bf),
            pltpu.VMEM((8192, 128), bf),
            pltpu.VMEM((32, 64, 256), bf),
            pltpu.VMEM((32, 64, 256), bf),
            pltpu.VMEM((NZ, 8, 128), bf),
            pltpu.VMEM((TP, 8, 128), bf),
            pltpu.VMEM((2, 32, 128), bf),
            pltpu.VMEM((2, 32, 128), bf),
            pltpu.VMEM((32, 8, 128), bf),
            pltpu.VMEM((2, 16, 8, 128), bf),
            pltpu.VMEM((1, 64), jnp.int32),
            pltpu.VMEM((1, 64), jnp.int32),
            pltpu.VMEM((64, 128), jnp.float32),
            pltpu.VMEM((NZ * 8, 64), bf),
            pltpu.VMEM((NZ * 8, 64), bf),
            pltpu.VMEM((128, 128), jnp.float32),
            pltpu.VMEM((2, 16, 8, 128), jnp.float32),
            pltpu.VMEM((2, 16, 8, 128), jnp.float32),
            pltpu.VMEM((2, 16, 8, 128), jnp.float32),
            pltpu.SMEM((64,), jnp.int32),
            pltpu.SMEM((TP,), jnp.int32),
            dma((9,)),
            dma((2,)),
            dma((2,)),
            dma((64,)),
            dma((64,)),
            dma((31,)),
            dma((31,)),
            dma((15,)),
            dma((15,)),
            dma,
            dma,
            dma,
            dma,
            pltpu.SemaphoreType.REGULAR((4,)),
        ],
        compiler_params=pltpu.CompilerParams(
            collective_id=0, has_side_effects=True, vmem_limit_bytes=24 * 1024 * 1024
        ),
        cost_estimate=pl.CostEstimate(
            flops=2 * 128 * 8192 * 128, bytes_accessed=5 * 1024 * 1024, transcendentals=0
        ),
    )(
        *(
            pltpu.with_memory_space_constraint(array, pltpu.HBM)
            for array in (
                hidden_old,
                queries_old,
                kv_weight,
                cache,
                lengths.reshape(1, 64),
                slot.reshape(1, 64),
                slot,
                hidden_new,
                queries_new.reshape(2, 16, 8, 128),
            )
        )
    )
    attended_old, attended_new, served = pl.pallas_call(
        hand_over,
        out_shape=tuple(jax.ShapeDtypeStruct(part.shape, part.dtype) for part in parts),
        in_specs=[any_spec] * 3,
        out_specs=(any_spec,) * 3,
        scratch_shapes=[dma((3,))],
        compiler_params=pltpu.CompilerParams(vmem_limit_bytes=16 * 1024 * 1024),
        cost_estimate=pl.CostEstimate(flops=0, bytes_accessed=2400000, transcendentals=0),
    )(*parts)
    return attended_old, attended_new, served.reshape(2, 1024, 256)


def solution(mesh):
    placed = (
        P(None, "rep", "tp"),
        P(("rep", "tp"), None, None),
        P(None, "tp"),
        P(("rep", "tp"), None, None),
        P("rep"),
        P("rep"),
        P(None, "rep", "tp"),
        P(("rep", "tp"), None, None),
    )
    return jax.shard_map(
        shards,
        mesh=mesh,
        in_specs=placed,
        out_specs=(
            P(("rep", "tp"), None, None),
            P(("rep", "tp"), None, None),
            P(("rep", "tp"), None, None),
        ),
        check_vma=False,
    )
```

```python
import jax
import jax.numpy as jnp
from jax import lax
from jax.experimental import pallas as pl
from jax.experimental.pallas import tpu as pltpu
from jax.sharding import PartitionSpec as P

MESH = pl.DeviceIdType.MESH
TP = 32
NZ = 16
SCALE = 1.0 / 128.0**0.5


def remote(src, dst, send_sem, recv_sem, target):
    return pltpu.make_async_remote_copy(
        src_ref=src,
        dst_ref=dst,
        send_sem=send_sem,
        recv_sem=recv_sem,
        device_id={"tp": target},
        device_id_type=MESH,
    )


def stored_part(queries, block, limit):
    keys = block[:, :, :128]
    values = block[:, :, 128:]
    scores = (
        jnp.einsum("egd,eld->egl", queries, keys, preferred_element_type=jnp.float32) * SCALE
    )
    position = lax.broadcasted_iota(jnp.int32, scores.shape, 2).astype(jnp.float32)
    scores = jnp.where(position < limit, scores, -jnp.inf)
    top = jnp.max(scores, axis=-1, keepdims=True)
    weights = jnp.exp(scores - top)
    total = jnp.sum(weights, axis=-1, keepdims=True)
    mixed = jnp.einsum(
        "egl,eld->egd", weights.astype(jnp.bfloat16), values, preferred_element_type=jnp.float32
    )
    return mixed, top, total


def with_tokens(queries, stored, tokens):
    mixed, top, total = stored
    query_f = queries.astype(jnp.float32)
    own = [jnp.sum(query_f * key, axis=-1, keepdims=True) * SCALE for key, _ in tokens]
    peak = top
    for score in own:
        peak = jnp.maximum(peak, score)
    shrink = jnp.exp(top - peak)
    mixed = mixed * shrink
    total = total * shrink
    for score, (_, value) in zip(own, tokens):
        weight = jnp.exp(score - peak)
        mixed = mixed + weight * value
        total = total + weight
    return mixed / total


def step_kernel(
    hold_hbm,
    qold_hbm,
    w_hbm,
    cache_hbm,
    len_hbm,
    slot_hbm,
    slot1_hbm,
    hnew_hbm,
    qnew_hbm,
    old_ref,
    new_ref,
    served_ref,
    hbuf,
    wbuf,
    cbuf,
    sbuf,
    mbuf,
    fbuf,
    obuf,
    pbuf,
    qobuf,
    qnbuf,
    len_row,
    slot_row,
    len_cols,
    pick_old,
    pick_new,
    acc,
    mixed_buf,
    top_buf,
    total_buf,
    slot_s,
    order_s,
    local_sem,
    xs_sem,
    xr_sem,
    gs_sem,
    gr_sem,
    cs_sem,
    cr_sem,
    ms_sem,
    mr_sem,
    ps_sem,
    pr_sem,
    ys_sem,
    yr_sem,
    near_sem,
):
    me = lax.axis_index("tp")
    x = me // NZ
    z = me % NZ
    other = 1 - x
    half = z % 2
    head = me // 2

    def on_ring(dz):
        return x * NZ + (z + dz) % NZ

    right, left, twin = on_ring(1), on_ring(NZ - 1), other * NZ + z
    barrier = pltpu.get_barrier_semaphore()
    for peer in (right, left, twin):
        pl.semaphore_signal(barrier, inc=1, device_id={"tp": peer}, device_id_type=MESH)

    loads = [
        (slot1_hbm, slot_s),
        (hold_hbm.at[x], hbuf.at[z, x, 0]),
        (hnew_hbm.at[x], hbuf.at[z, x, 1]),
        (slot_hbm, slot_row),
        (len_hbm, len_row),
        (cache_hbm, cbuf),
        (w_hbm, wbuf),
        (qold_hbm, qobuf),
        (qnew_hbm, qnbuf),
    ]
    loads = [
        pltpu.make_async_copy(src, dst, local_sem.at[i]) for i, (src, dst) in enumerate(loads)
    ]
    for c in loads:
        c.start()
    for c in loads[1:3]:
        c.wait()

    pl.semaphore_wait(barrier, 3)

    xcopies = []
    for p, src in enumerate((hold_hbm, hnew_hbm)):
        c = remote(src.at[other], hbuf.at[z, x, p], xs_sem.at[p], xr_sem.at[p], twin)
        c.start()
        xcopies.append(c)

    steps = ((8, 7), (7, 8))
    planes = (x, other)
    sent = []

    def ring(stream, way, k, p):
        slot = (z + (NZ - k if way == 0 else k)) % NZ
        block = hbuf.at[slot, planes[stream], p]
        where = ((stream * 2 + way) * 8 + k) * 2 + p
        return remote(block, block, gs_sem.at[where], gr_sem.at[where], right if way == 0 else left)

    def forward(stream, way, k, p):
        c = ring(stream, way, k, p)
        c.start()
        sent.append(c)

    for p in range(2):
        for way in range(2):
            forward(0, way, 0, p)

    def greet(i, dist):
        for way, dz in ((0, dist), (1, NZ - dist)):
            pl.semaphore_signal(
                near_sem.at[2 * i + way],
                inc=1,
                device_id={"tp": on_ring(dz)},
                device_id_type=MESH,
            )

    def greeted(i):
        for way in range(2):
            pl.semaphore_wait(near_sem.at[2 * i + way], 1)

    loads[0].wait()

    def find(u, carry):
        found = 0
        for r in range(32):
            found = jnp.where(slot_s[32 * half + r] == 2 * u + half, r, found)
        order_s[u] = found
        return carry

    lax.fori_loop(0, TP, find, 0)
    for c in loads[3:5]:
        c.wait()
    for p in range(2):
        xcopies[p].wait_recv()
        for way in range(2):
            forward(1, way, 0, p)

    acc[...] = jnp.zeros_like(acc)
    rid = lax.broadcasted_iota(jnp.int32, (NZ * 8, 64), 0)
    col = lax.broadcasted_iota(jnp.int32, (NZ * 8, 64), 1)
    j = rid & 3
    plane = jnp.where((rid & 7) < 4, x, other)
    row = 2 * (plane * NZ + (rid >> 3)) + (j & 1)
    pick_old[...] = (
        (slot_row[...] == jnp.where(j < 2, row, -1)).astype(jnp.float32).astype(jnp.bfloat16)
    )
    pick_new[...] = (col == jnp.where(j < 2, -1, row)).astype(jnp.float32).astype(jnp.bfloat16)
    eye = lax.broadcasted_iota(jnp.int32, (64, 64), 0) == lax.broadcasted_iota(
        jnp.int32, (64, 64), 1
    )
    lengths_f = len_row[...].astype(jnp.float32)
    column = jnp.sum(jnp.where(eye, lengths_f, 0.0), axis=1, keepdims=True)
    len_cols[...] = jnp.broadcast_to(column, (64, 128))

    loads[5].wait()

    order = [(0, 8)]
    for dz in range(7, 0, -1):
        order += [(0, dz), (1, dz), (0, NZ - dz), (1, NZ - dz)]
    order += [(1, 0), (1, 8)]
    cache_copies = []

    def send_blocks(count):
        for _ in range(count):
            i = len(cache_copies)
            if i == len(order):
                return
            dx, dz = order[i]
            target = (x + dx) % 2 * NZ + (z + dz) % NZ
            sbuf[i] = cbuf[order_s[target]]
            c = remote(
                sbuf.at[i], served_ref.at[half, head], cs_sem.at[i], cr_sem.at[i], target
            )
            c.start()
            cache_copies.append(c)

    def multiply(stream, slot):
        plane = planes[stream]
        rows = pl.ds(pl.multiple_of((plane * NZ + slot) * 256, 256), 256)
        acc[...] += jnp.dot(
            hbuf[slot, plane].reshape(128, 256), wbuf[rows, :], preferred_element_type=jnp.float32
        )

    loads[6].wait()
    for k in range(8):
        for stream in range(2):
            for p in range(2):
                for way in range(2):
                    if k >= steps[stream][way]:
                        continue
                    ring(stream, way, k, p).wait_recv()
                    if k + 1 < steps[stream][way]:
                        forward(stream, way, k + 1, p)
        if k == 0:
            greet(0, 2)
        elif k == 1:
            greeted(0)
            greet(1, 4)
        elif k == 2:
            greeted(1)
        send_blocks((0, 0, 6, 4, 4, 3, 2, 1)[k])
        if k == 0:
            multiply(0, z)
            multiply(1, z)
        for stream in range(2):
            for way in range(2):
                if k < steps[stream][way]:
                    multiply(stream, (z + (NZ - k - 1 if way == 0 else k + 1)) % NZ)

    fresh = acc[...].astype(jnp.bfloat16)
    obuf[...] = fresh[:64].reshape(2, 32, 128)
    partner = on_ring(NZ + 1 - 2 * half)
    pcopy = remote(obuf.at[1 - half], pbuf.at[half], ps_sem, pr_sem, partner)
    pcopy.start()
    messages = jnp.dot(pick_old[...], fresh[:64], preferred_element_type=jnp.float32) + jnp.dot(
        pick_new[...], fresh[64:], preferred_element_type=jnp.float32
    )
    mbuf[...] = messages.astype(jnp.bfloat16).reshape(NZ, 8, 128)
    message_copies = []
    for i, dz in enumerate((8, 7, 9, 6, 10, 5, 11, 4, 12, 3, 13, 2, 14, 1, 15)):
        c = remote(
            mbuf.at[(z + dz) % NZ], fbuf.at[me], ms_sem.at[i], mr_sem.at[i], on_ring(dz)
        )
        c.start()
        message_copies.append(c)
    send_blocks(31)
    pbuf[half] = obuf[half]
    fbuf[me] = mbuf[z]
    served_ref[half, head] = cbuf[order_s[me]]

    loads[7].wait()
    loads[8].wait()
    stored_old = []
    for c in range(2):
        entries = pl.ds(16 * c, 16)
        limit = len_cols[pl.ds(pl.multiple_of(32 * half + 16 * c, 16), 16), :][:, None, :64]
        stored_old.append(stored_part(qobuf[entries], cbuf[entries], limit))
    pcopy.wait()
    for c in range(2):
        entries = pl.ds(16 * c, 16)
        tokens = [
            (
                pbuf[0, entries].astype(jnp.float32)[:, None, :],
                pbuf[1, entries].astype(jnp.float32)[:, None, :],
            )
        ]
        old_ref[entries] = with_tokens(qobuf[entries], stored_old[c], tokens).astype(jnp.bfloat16)

    for c in message_copies:
        c.wait()
    ring_rows = fbuf.at[pl.ds(pl.multiple_of(x * NZ, NZ), NZ)]
    relay = remote(ring_rows, ring_rows, ys_sem, yr_sem, twin)
    relay.start()
    new_len = []
    for p in range(2):
        count = jnp.sum(
            jnp.where(slot_row[...] == 2 * me + p, lengths_f, 0.0), axis=1, keepdims=True
        )
        new_len.append(count.reshape(1, 1, 1))

    def arrived(group):
        places = []
        for i in group:
            if i < len(order):
                cache_copies[i].wait_recv()
                dx, dz = order[i]
                zs = (z + NZ - dz) % NZ
                places.append((zs % 2, ((x + dx) % 2 * NZ + zs) // 2))
            else:
                places.append((half, head))
        queries = jnp.stack(
            [qnbuf[h, a] for h, a in places]
        )
        blocks = jnp.stack([served_ref[h, a] for h, a in places])
        limit = jnp.concatenate(
            [jnp.where(h == 0, new_len[0], new_len[1]) for h, _ in places], axis=0
        )
        mixed, top, total = stored_part(queries, blocks, limit)
        for n, (h, a) in enumerate(places):
            mixed_buf[h, a] = mixed[n]
            top_buf[h, a] = jnp.broadcast_to(top[n], (8, 128))
            total_buf[h, a] = jnp.broadcast_to(total[n], (8, 128))

    for g in range(4):
        arrived(range(8 * g, 8 * g + 8))
    relay.wait()
    received = fbuf[...].astype(jnp.float32).reshape(16, 2, 8, 128)
    mine = (lax.broadcasted_iota(jnp.int32, (16, 1, 128), 0) >> 3) == x

    def token_row(kind, j):
        return jnp.where(mine, received[:, kind, j : j + 1], received[:, kind, j + 4 : j + 5])

    for p in range(2):
        queries = qnbuf[p]
        first_key, first_value = token_row(0, p), token_row(1, p)
        tokens = [(first_key, first_value), (token_row(0, p + 2), token_row(1, p + 2))]
        stored = (mixed_buf[p], top_buf[p][:, :, :1], total_buf[p][:, :, :1])
        attended = with_tokens(queries, stored, tokens)
        new_ref[p] = attended.astype(jnp.bfloat16).reshape(128, 128)
        row = lax.broadcasted_iota(jnp.int32, (1, 64, 256), 1).astype(jnp.float32)
        token = jnp.concatenate([first_key, first_value], axis=2)
        served_ref[p] = jnp.where(
            row == new_len[p], token, served_ref[p].astype(jnp.float32)
        ).astype(jnp.bfloat16)

    for c in cache_copies:
        c.wait_send()
    for c in sent:
        c.wait_send()
    for c in xcopies:
        c.wait_send()


def hand_over(old_in, new_in, served_in, old_ref, new_ref, served_ref, sem):
    copies = [
        pltpu.make_async_copy(served_in, served_ref, sem.at[0]),
        pltpu.make_async_copy(old_in, old_ref, sem.at[1]),
        pltpu.make_async_copy(new_in, new_ref, sem.at[2]),
    ]
    for c in copies:
        c.start()
    for c in copies:
        c.wait()


def shards(hidden_old, queries_old, kv_weight, cache, lengths, slot, hidden_new, queries_new):
    hbm = pl.BlockSpec(memory_space=pltpu.HBM)
    any_spec = pl.BlockSpec(memory_space=pl.ANY)
    vmem = pl.BlockSpec(memory_space=pltpu.VMEM)
    dma = pltpu.SemaphoreType.DMA
    bf = jnp.bfloat16
    parts = pl.pallas_call(
        step_kernel,
        out_shape=(
            jax.ShapeDtypeStruct((32, 8, 128), bf),
            jax.ShapeDtypeStruct((2, 128, 128), bf),
            jax.ShapeDtypeStruct((2, 16, 64, 256), bf),
        ),
        in_specs=[hbm] * 9,
        out_specs=(vmem, vmem, vmem),
        scratch_shapes=[
            pltpu.VMEM((NZ, 2, 2, 64, 256), bf),
            pltpu.VMEM((8192, 128), bf),
            pltpu.VMEM((32, 64, 256), bf),
            pltpu.VMEM((32, 64, 256), bf),
            pltpu.VMEM((NZ, 8, 128), bf),
            pltpu.VMEM((TP, 8, 128), bf),
            pltpu.VMEM((2, 32, 128), bf),
            pltpu.VMEM((2, 32, 128), bf),
            pltpu.VMEM((32, 8, 128), bf),
            pltpu.VMEM((2, 16, 8, 128), bf),
            pltpu.VMEM((1, 64), jnp.int32),
            pltpu.VMEM((1, 64), jnp.int32),
            pltpu.VMEM((64, 128), jnp.float32),
            pltpu.VMEM((NZ * 8, 64), bf),
            pltpu.VMEM((NZ * 8, 64), bf),
            pltpu.VMEM((128, 128), jnp.float32),
            pltpu.VMEM((2, 16, 8, 128), jnp.float32),
            pltpu.VMEM((2, 16, 8, 128), jnp.float32),
            pltpu.VMEM((2, 16, 8, 128), jnp.float32),
            pltpu.SMEM((64,), jnp.int32),
            pltpu.SMEM((TP,), jnp.int32),
            dma((9,)),
            dma((2,)),
            dma((2,)),
            dma((64,)),
            dma((64,)),
            dma((31,)),
            dma((31,)),
            dma((15,)),
            dma((15,)),
            dma,
            dma,
            dma,
            dma,
            pltpu.SemaphoreType.REGULAR((4,)),
        ],
        compiler_params=pltpu.CompilerParams(
            collective_id=0, has_side_effects=True, vmem_limit_bytes=24 * 1024 * 1024
        ),
        cost_estimate=pl.CostEstimate(
            flops=2 * 128 * 8192 * 128, bytes_accessed=5 * 1024 * 1024, transcendentals=0
        ),
    )(
        *(
            pltpu.with_memory_space_constraint(array, pltpu.HBM)
            for array in (
                hidden_old,
                queries_old,
                kv_weight,
                cache,
                lengths.reshape(1, 64),
                slot.reshape(1, 64),
                slot,
                hidden_new,
                queries_new.reshape(2, 16, 8, 128),
            )
        )
    )
    attended_old, attended_new, served = pl.pallas_call(
        hand_over,
        out_shape=tuple(jax.ShapeDtypeStruct(part.shape, part.dtype) for part in parts),
        in_specs=[any_spec] * 3,
        out_specs=(any_spec,) * 3,
        scratch_shapes=[dma((3,))],
        compiler_params=pltpu.CompilerParams(vmem_limit_bytes=16 * 1024 * 1024),
        cost_estimate=pl.CostEstimate(flops=0, bytes_accessed=2400000, transcendentals=0),
    )(*parts)
    return attended_old, attended_new, served.reshape(2, 1024, 256)


def solution(mesh):
    placed = (
        P(None, "rep", "tp"),
        P(("rep", "tp"), None, None),
        P(None, "tp"),
        P(("rep", "tp"), None, None),
        P("rep"),
        P("rep"),
        P(None, "rep", "tp"),
        P(("rep", "tp"), None, None),
    )
    return jax.shard_map(
        shards,
        mesh=mesh,
        in_specs=placed,
        out_specs=(
            P(("rep", "tp"), None, None),
            P(("rep", "tp"), None, None),
            P(("rep", "tp"), None, None),
        ),
        check_vma=False,
    )
```
